256 devices in a mesh: gx: 4 (over z_hi), gy: 8 (over y, core), gz: 8 (over z_lo, x).
Axes of the slice: x: 4, y: 4, z: 8 (z_hi: 4, z_lo: 2; z = z_hi * 2 + z_lo), core: 2. Of those that a mesh axis runs over, the one named last changes fastest.
Arguments:
- terminal_cost_cotangent: float32 [8, 216, 32768], P(None, None, ('gx', 'gy', 'gz')), may hold values from -6 to 6
- stored_section_populations: bfloat16 [2, 8, 216, 32768], P(None, None, None, ('gx', 'gy', 'gz')), may hold values from -6 to 6
- pairwise_collision_rates: float32 [8, 8, 8], replicated, may hold values from -1 to 1
- liquid_motion_field: float32 [3, 32768], P(None, ('gx', 'gy', 'gz')), may hold values from -3 to 3
- class_ascent_drift: float32 [8], replicated, may hold values from 0.2 to 1
- sparger_inlet_flags: int32 [8, 64], P('gx', 'gy'), may hold values 0 or 1
Outputs:
- initial_adjoint: float32 [8, 216, 32768], P(None, None, ('gx', 'gy', 'gz'))
The draws below stay inside these ranges and needn't reach their ends.
All inputs are finite; a program needn't handle non-finite values. No bound on the sum of `sparger_inlet_flags` on one device may be relied on, other than what follows from the above.
Results may differ from the reference program's by a relative error of at most 0.0003.
Values sent between devices are 32-bit elements; how exact they have to be, the bound alone decides.
A program may use at most 64 MiB of HBM per device.

```python
import math
import jax
import jax.numpy as jnp
import numpy as np
from jax import lax

BUBBLE_BINS = 8
EX = 2
EY = 8
EZ = 8
WIDTH_ELEMENTS = 8
DEPTH_ELEMENTS = 64
HEIGHT_ELEMENTS = 64
MESH_CELL_TOTAL = 32768
N_GX = 4
N_GY = 8
N_GZ = 8


def with_ends(drawn, own_key, least, top_value):
    longest = drawn.shape.index(max(drawn.shape))
    spots = []
    for shift in (0, 1):
        where = [jax.random.randint(jax.random.fold_in(own_key, axis), (), 0, length) for axis, length in enumerate(drawn.shape)]
        where[longest] = (where[longest] + shift) % drawn.shape[longest]
        spots.append(tuple(where))
    return drawn.at[spots[0]].set(least).at[spots[1]].set(top_value)


def level_of(key, shape, shards, least, top_value):
    level = 1.0
    for axis_at, blocks in shards:
        steps = jax.random.uniform(jax.random.fold_in(jax.random.fold_in(key, 6), axis_at), (blocks,), jnp.float32, least / len(shards), top_value / len(shards))
        level = level * jnp.repeat(jnp.exp(steps), shape[axis_at] // blocks).reshape((-1,) + (1,) * (len(shape) - 1 - axis_at))
    return level


def centred(key, dims, width, limit, pieces=(), held_as=jnp.bfloat16):
    entries = width * jax.random.normal(key, dims, jnp.float32)
    if pieces:
        entries = entries * level_of(key, dims, pieces, -0.22, 0.18)
    return jnp.clip(entries, -limit, limit).astype(held_as)


def setup_inputs(seed: int = 0) -> dict:
    keys = jax.random.split(jax.random.key(seed), 7)
    terminal_cost_cotangent = centred(keys[0], (BUBBLE_BINS, 216, MESH_CELL_TOTAL), 1.0, 6.0, ((2, 256),), jnp.float32)
    stored_section_populations = centred(keys[1], (2, BUBBLE_BINS, 216, MESH_CELL_TOTAL), 1.0, 6.0, ((3, 256),))
    pairwise_collision_rates = centred(keys[2], (BUBBLE_BINS, BUBBLE_BINS, BUBBLE_BINS), 0.2, 1.0, (), jnp.float32)
    liquid_motion_field = centred(keys[3], (3, MESH_CELL_TOTAL), 0.5, 3.0, ((1, 256),), jnp.float32)
    class_ascent_drift = jnp.clip(jnp.exp(jax.random.uniform(keys[4], (BUBBLE_BINS,), jnp.float32, math.log(0.2), math.log(1.0))), 0.2, 1.0)
    sparger_inlet_flags = with_ends((jax.random.randint(keys[5], (WIDTH_ELEMENTS, DEPTH_ELEMENTS), 0, 2) < 1).astype(jnp.int32), jax.random.fold_in(keys[5], 1), 0, 1)
    return {"terminal_cost_cotangent": terminal_cost_cotangent, "stored_section_populations": stored_section_populations, "pairwise_collision_rates": pairwise_collision_rates, "liquid_motion_field": liquid_motion_field, "class_ascent_drift": class_ascent_drift, "sparger_inlet_flags": sparger_inlet_flags}


STEP_LENGTH = 0.05


def derivative_table():
    points = np.array([-1.0, -0.765055323929465, -0.285231516480645, 0.285231516480645, 0.765055323929465, 1.0])
    legendre = (63.0 * points ** 5 - 70.0 * points ** 3 + 15.0 * points) / 8.0
    matrix = np.zeros((6, 6))
    for row_index in range(6):
        for col_index in range(6):
            if row_index != col_index:
                matrix[row_index, col_index] = legendre[row_index] / legendre[col_index] / (points[row_index] - points[col_index])
    matrix[0, 0] = -7.5
    matrix[5, 5] = 7.5
    return jnp.asarray(matrix, dtype=jnp.float32)


def pair_sum(padded, direction):
    extent = padded.shape[direction] - 2
    middle = lax.slice_in_dim(padded, 1, extent + 1, axis=direction)
    upper_cells = lax.slice_in_dim(padded, 2, extent + 2, axis=direction)
    lower_cells = lax.slice_in_dim(padded, 0, extent, axis=direction)
    layout = [1] * padded.ndim
    layout[direction] = extent
    position = (jnp.arange(extent) % 6).reshape(layout)
    return middle + jnp.where(position == 5, upper_cells, 0.0) + jnp.where(position == 0, lower_cells, 0.0)


def to_grid(values):
    block_list = values.reshape(6, 6, 6, N_GX, N_GY, N_GZ, EX, EY, EZ)
    block_list = block_list.transpose(3, 6, 0, 4, 7, 1, 5, 8, 2)
    return block_list.reshape(6 * WIDTH_ELEMENTS, 6 * DEPTH_ELEMENTS, 6 * HEIGHT_ELEMENTS)


def from_grid(grid):
    block_list = grid.reshape(N_GX, EX, 6, N_GY, EY, 6, N_GZ, EZ, 6)
    block_list = block_list.transpose(2, 5, 8, 0, 3, 6, 1, 4, 7)
    return block_list.reshape(216, MESH_CELL_TOTAL)


def assemble(field, keep):
    def one_class(values):
        grid = jnp.pad(to_grid(values * keep), 1)
        for direction in range(3):
            grid = pair_sum(grid, direction)
        return from_grid(grid)
    return lax.map(one_class, field)


def adjoint_operator(adjoint, state, integration_factors, pace_magnitude, matrix):
    highest = lax.Precision.HIGHEST

    def one_class(inputs):
        values, class_speed = inputs
        cube = values.reshape(6, 6, 6, MESH_CELL_TOTAL)
        along_x = jnp.einsum('im,ijke->mjke', matrix, cube, precision=highest)
        along_y = jnp.einsum('jm,ijke->imke', matrix, cube, precision=highest)
        along_z = jnp.einsum('km,ijke->ijme', matrix, cube, precision=highest)
        total = class_speed[0] * along_x + class_speed[1] * along_y + class_speed[2] * along_z
        return -total.reshape(216, MESH_CELL_TOTAL)

    advective = lax.map(one_class, (adjoint, pace_magnitude))
    flat_adjoint = adjoint.reshape(BUBBLE_BINS, -1)
    flat_state = state.reshape(BUBBLE_BINS, -1)
    rotated = integration_factors.transpose(1, 2, 0)

    def one_target(rates):
        return jnp.sum(flat_state * jnp.dot(rates, flat_adjoint, precision=highest), axis=0)

    coupling = lax.map(one_target, rotated).reshape(BUBBLE_BINS, 216, MESH_CELL_TOTAL)
    return advective + coupling


def reference(terminal_cost_cotangent, stored_section_populations, pairwise_collision_rates, liquid_motion_field, class_ascent_drift, sparger_inlet_flags):
    matrix = derivative_table()
    flags = sparger_inlet_flags.reshape(N_GX, EX, N_GY, EY).transpose(0, 2, 1, 3)
    flags = flags[:, :, None, :, :, None] == 1
    layer_gz = (jnp.arange(N_GZ) == 0)[None, None, :, None, None, None]
    layer_ez = (jnp.arange(EZ) == 0)[None, None, None, None, None, :]
    bottom = jnp.broadcast_to(flags & layer_gz & layer_ez, (N_GX, N_GY, N_GZ, EX, EY, EZ)).reshape(MESH_CELL_TOTAL)
    node_low = (jnp.arange(216) % 6) == 0
    keep = jnp.where(node_low[:, None] & bottom[None, :], 0.0, 1.0).astype(jnp.float32)
    integration_factors = pairwise_collision_rates + pairwise_collision_rates.transpose(0, 2, 1)
    vertical_scale = jnp.array([0.0, 0.0, 1.0], dtype=jnp.float32)
    pace_magnitude = liquid_motion_field[None, :, :] + class_ascent_drift[:, None, None] * vertical_scale[None, :, None]
    states = stored_section_populations.astype(jnp.float32)
    final_adjoint = assemble(terminal_cost_cotangent, keep)
    late_term = adjoint_operator(final_adjoint, states[1], integration_factors, pace_magnitude, matrix)
    middle_adjoint = 0.5 * (final_adjoint + STEP_LENGTH * assemble(late_term, keep))
    early_term = adjoint_operator(middle_adjoint, states[0], integration_factors, pace_magnitude, matrix)
    return 0.5 * final_adjoint + middle_adjoint + STEP_LENGTH * assemble(early_term, keep)
```

```python
import functools

import jax
import jax.numpy as jnp
import numpy as np
from jax import lax
from jax.experimental import pallas as pl
from jax.experimental.pallas import tpu as pltpu
from jax.sharding import PartitionSpec as P

EX = 2
EY = 8
EZ = 8
STEP_LENGTH = 0.05
AXES = ("gx", "gy", "gz")
STRIDES = (36, 6, 1)
MESH = pl.DeviceIdType.MESH
NODES = 216
F32 = jnp.float32


def derivative_numbers():
    points = np.array(
        [-1.0, -0.765055323929465, -0.285231516480645, 0.285231516480645, 0.765055323929465, 1.0]
    )
    legendre = (63.0 * points**5 - 70.0 * points**3 + 15.0 * points) / 8.0
    matrix = np.zeros((6, 6))
    for row_index in range(6):
        for col_index in range(6):
            if row_index != col_index:
                matrix[row_index, col_index] = (
                    legendre[row_index]
                    / legendre[col_index]
                    / (points[row_index] - points[col_index])
                )
    matrix[0, 0] = -7.5
    matrix[5, 5] = 7.5
    return matrix


DMAT = derivative_numbers()
EVEN = [[0.5 * float(DMAT[i, m] + DMAT[5 - i, m]) for m in range(3)] for i in range(3)]
ODD = [[0.5 * float(DMAT[i, m] - DMAT[5 - i, m]) for m in range(3)] for i in range(3)]

INNER = [(a, b) for a in range(1, 5) for b in range(1, 5)]
Y_GROUPS = [
    [(0, k) for k in range(6)] + INNER[0:2],
    [(5, k) for k in range(6)] + INNER[2:4],
    [(i, 0) for i in range(6)] + INNER[4:6],
    [(i, 5) for i in range(6)] + INNER[6:8],
    INNER[8:16],
]
REST = [(i, j) for i in range(1, 5) for j in range(6)]
Z_GROUPS = [
    [(0, j) for j in range(6)] + REST[0:2],
    [(5, j) for j in range(6)] + REST[2:4],
    REST[4:12],
    REST[12:20],
    REST[20:24],
]
XL, XH, YL, YH, ZL, ZH, SEND_TILES = 0, 18, 36, 41, 46, 51, 56


def source_of(d):
    dx, dy, dz = d
    if dy == 0 and dz == 0:
        return (XL if dx < 0 else XH), 18
    if dx == 0 and dz == 0:
        return (YL if dy < 0 else YH), 5
    if dx == 0 and dy == 0:
        return (ZL if dz < 0 else ZH), 5
    if dy == 0:
        return (ZL if dz < 0 else ZH) + (0 if dx < 0 else 1), 1
    if dx != 0:
        return (YL if dy < 0 else YH) + (0 if dx < 0 else 1), 1
    return (YL if dy < 0 else YH) + (2 if dz < 0 else 3), 1


def directions():
    every = [(x, y, z) for x in (-1, 0, 1) for y in (-1, 0, 1) for z in (-1, 0, 1) if (x, y, z) != (0, 0, 0)]

    def rank(d):
        count = sum(abs(v) for v in d)
        if count == 3:
            return 0
        if count == 2:
            return 1 if d[1] == 0 else (2 if d[2] == 0 else 3)
        return 4 if d[2] else (5 if d[1] else 6)

    return sorted(every, key=rank)


DIRECTIONS = directions()
RECV_AT = {}
RECV_TILES = 0
for _d in DIRECTIONS:
    RECV_AT[_d] = RECV_TILES
    RECV_TILES += source_of(_d)[1]


def roll(x, shift):
    shift = shift % 128
    return x if shift == 0 else pltpu.roll(x, shift, 1)


def exists(d, sizes):
    ok = None
    for axis, off, size in zip(AXES, d, sizes):
        if off == 0:
            continue
        here = lax.axis_index(axis)
        term = here < size - 1 if off > 0 else here > 0
        ok = term if ok is None else jnp.logical_and(ok, term)
    return ok


def device_at(d):
    return {axis: lax.axis_index(axis) + off for axis, off in zip(AXES, d) if off != 0}


def kernel(
    sizes, cost_hbm, state_hbm, rates_hbm, motion_hbm, drift_hbm, flags_hbm, out_ref,
    drift_ref, flags_ref, stage, state_v, state_f, rates_v, motion_v, mix_lhs, mix, X, T, consts,
    send_buf, recv_buf, send_sem, recv_sem, load_sem,
):
    lane = lax.broadcasted_iota(jnp.int32, (8, 128), 1)
    sub = lax.broadcasted_iota(jnp.int32, (8, 128), 0)
    p_at, q_at, r_at = lane // 64, (lane // 8) % 8, lane % 8

    loads = [
        pltpu.make_async_copy(cost_hbm, stage, load_sem.at[0]),
        pltpu.make_async_copy(motion_hbm, motion_v, load_sem.at[1]),
        pltpu.make_async_copy(rates_hbm, rates_v, load_sem.at[2]),
        pltpu.make_async_copy(state_hbm, state_v, load_sem.at[3]),
        pltpu.make_async_copy(drift_hbm, drift_ref, load_sem.at[4]),
        pltpu.make_async_copy(flags_hbm, flags_ref, load_sem.at[5]),
    ]
    for load in loads:
        load.start()

    barrier = pltpu.get_barrier_semaphore()
    for d in DIRECTIONS:
        @pl.when(exists(d, sizes))
        def _():
            pl.semaphore_signal(barrier, inc=1, device_id=device_at(d), device_id_type=MESH)

    for d in DIRECTIONS:
        n = source_of(d)[1]

        @pl.when(jnp.logical_not(exists(tuple(-v for v in d), sizes)))
        def _():
            for s in range(3):
                recv_buf[s, pl.ds(RECV_AT[d], n)] = jnp.zeros((n, 8, 128), F32)

    loads[5].wait()
    keep = jnp.ones((8, 128), F32)
    bottom = lax.axis_index("gz") == 0
    for p in range(EX):
        for q in range(EY):
            open_here = 1.0 - flags_ref[p, q].astype(F32)
            hit = jnp.logical_and(lane == p * 64 + q * 8, bottom)
            keep = jnp.where(hit, open_here, keep)
    consts[0] = keep

    def sweep(ref, d):
        a_d, b_d = [x for x in range(3) if x != d]
        shift = (64, 8, 1)[d]
        at = (p_at, q_at, r_at)[d]
        last = (1, 7, 7)[d]

        def body(t, _):
            for u in range(6):
                lo_n = t * STRIDES[a_d] + u * STRIDES[b_d]
                hi_n = lo_n + 5 * STRIDES[d]
                a, b = ref[lo_n], ref[hi_n]
                if d == 0:
                    both = jnp.where(at == 1, a, b)
                    both = both + roll(both, 64)
                    ref[lo_n] = jnp.where(at == 1, both, a)
                    ref[hi_n] = jnp.where(at == 0, both, b)
                else:
                    s = a + roll(b, shift)
                    ref[lo_n] = jnp.where(at > 0, s, a)
                    ref[hi_n] = jnp.where(at < last, roll(s, -shift), b)
            return 0

        lax.fori_loop(0, 6, body, 0)

    def pack(slot):
        for g, group in enumerate(Y_GROUPS):
            low = high = jnp.zeros((8, 128), F32)
            for s, (i, k) in enumerate(group):
                low = jnp.where(q_at == s, roll(T[i * 36 + k], 8 * s), low)
                high = jnp.where(q_at == s, roll(T[i * 36 + 30 + k], 8 * (s - 7)), high)
            send_buf[slot, YL + g] = low
            send_buf[slot, YH + g] = high
        for g, group in enumerate(Z_GROUPS):
            low = high = jnp.zeros((8, 128), F32)
            for s, (i, j) in enumerate(group):
                low = jnp.where(r_at == s, roll(T[i * 36 + j * 6], s), low)
                high = jnp.where(r_at == s, roll(T[i * 36 + j * 6 + 5], s - 7), high)
            send_buf[slot, ZL + g] = low
            send_buf[slot, ZH + g] = high

        def body(t, _):
            for v in range(6):
                n = t * 6 + v
                send_buf[slot, XL + n] = jnp.where(p_at == 1, roll(T[n], 64), T[n + 18])
                send_buf[slot, XH + n] = jnp.where(p_at == 0, roll(T[180 + n], 64), T[180 + n + 18])
            return 0

        lax.fori_loop(0, 3, body, 0)

    def message(slot, m):
        d = DIRECTIONS[m]
        at, n = source_of(d)
        return pltpu.make_async_remote_copy(
            src_ref=send_buf.at[slot, pl.ds(at, n)],
            dst_ref=recv_buf.at[slot, pl.ds(RECV_AT[d], n)],
            send_sem=send_sem.at[slot, m],
            recv_sem=recv_sem.at[slot, m],
            device_id=device_at(d),
            device_id_type=MESH,
        )

    def start_all(slot):
        for m, d in enumerate(DIRECTIONS):
            @pl.when(exists(d, sizes))
            def _():
                message(slot, m).start()

    def wait_sent(slot):
        for m, d in enumerate(DIRECTIONS):
            @pl.when(exists(d, sizes))
            def _():
                message(slot, m).wait_send()

    def wait_received(slot):
        for m, d in enumerate(DIRECTIONS):
            @pl.when(exists(tuple(-v for v in d), sizes))
            def _():
                message(slot, m).wait_recv()

    def got(slot, f, tile=0):
        return recv_buf[slot, RECV_AT[tuple(-v for v in f)] + tile]

    def unpack(slot):
        zero = jnp.zeros((8, 128), F32)

        def body(t, _):
            for v in range(6):
                n = t * 6 + v
                above = recv_buf[slot, RECV_AT[(-1, 0, 0)] + n]
                below = recv_buf[slot, RECV_AT[(1, 0, 0)] + n]
                X[slot, 180 + n] += jnp.where(p_at == 1, above, zero)
                X[slot, 180 + n + 18] += jnp.where(p_at == 1, roll(above, 64), zero)
                X[slot, n] += jnp.where(p_at == 0, below, zero)
                X[slot, n + 18] += jnp.where(p_at == 0, roll(below, 64), zero)
            return 0

        lax.fori_loop(0, 3, body, 0)
        for fy in (1, -1):
            for g, group in enumerate(Y_GROUPS):
                v = got(slot, (0, fy, 0), g)
                if g in (0, 1):
                    fx = 1 if g == 1 else -1
                    mine = jnp.logical_and(p_at == (1 if fx > 0 else 0), q_at < 6)
                    v = v + jnp.where(mine, roll(got(slot, (fx, fy, 0)), 64), zero)
                    for fz in (1, -1):
                        target = (64 if fx > 0 else 0) + (47 if fz > 0 else 0)
                        origin = (0 if fx > 0 else 64) + (0 if fz > 0 else 47)
                        v = v + jnp.where(lane == target, roll(got(slot, (fx, fy, fz)), target - origin), zero)
                if g in (2, 3):
                    fz = 1 if g == 3 else -1
                    v = jnp.where(jnp.logical_or(q_at == 0, q_at == 5), zero, v)
                    mine = jnp.logical_and(r_at == (7 if fz > 0 else 0), q_at < 6)
                    v = v + jnp.where(mine, roll(got(slot, (0, fy, fz)), 7 * fz), zero)
                for s, (i, k) in enumerate(group):
                    if fy > 0:
                        n, piece = i * 36 + 30 + k, jnp.where(q_at == 7, roll(v, 8 * (7 - s)), zero)
                    else:
                        n, piece = i * 36 + k, jnp.where(q_at == 0, roll(v, -8 * s), zero)
                    X[slot, n] += piece
        for fz in (1, -1):
            for g, group in enumerate(Z_GROUPS):
                v = got(slot, (0, 0, fz), g)
                if g in (0, 1):
                    fx = 1 if g == 1 else -1
                    mine = jnp.logical_and(p_at == (1 if fx > 0 else 0), r_at < 6)
                    v = v + jnp.where(mine, roll(got(slot, (fx, 0, fz)), 64), zero)
                for s, (i, j) in enumerate(group):
                    if fz > 0:
                        n, piece = i * 36 + j * 6 + 5, jnp.where(r_at == 7, roll(v, 7 - s), zero)
                    else:
                        n, piece = i * 36 + j * 6, jnp.where(r_at == 0, roll(v, -s), zero)
                    X[slot, n] += piece

    def line(r, base, d, outputs, with_mix):
        stride = STRIDES[d]
        h = [X[r, base + m * stride] for m in range(6)]
        even = [h[i] + h[5 - i] for i in range(3)]
        odd = [h[i] - h[5 - i] for i in range(3)]
        speed = consts[1 + d]
        for m in range(3):
            if m not in outputs:
                continue
            pe = EVEN[0][m] * even[0] + EVEN[1][m] * even[1] + EVEN[2][m] * even[2]
            qo = ODD[0][m] * odd[0] + ODD[1][m] * odd[1] + ODD[2][m] * odd[2]
            for at, value in ((m, qo + pe), (5 - m, qo - pe)):
                n = base + at * stride
                value = speed * value
                if d > 0:
                    value = value + T[n]
                if with_mix:
                    for a in range(8):
                        value = value + mix[1 - r, n, pl.ds(8 * a, 8), :] * X[r, n, pl.ds(a, 1), :]
                    if at == 0:
                        value = value * consts[0]
                T[n] = value

    def operator(r, boundary):
        for d in range(3):
            a_d, b_d = [x for x in range(3) if x != d]
            sa, sb = STRIDES[a_d], STRIDES[b_d]
            mixed = d == 2
            if boundary:
                def face_a(t, _):
                    line(r, t * sb, d, (0, 1, 2), mixed)
                    line(r, t * sb + 5 * sa, d, (0, 1, 2), mixed)
                    return 0

                def face_b(t, _):
                    line(r, t * sa, d, (0, 1, 2), mixed)
                    line(r, t * sa + 5 * sb, d, (0, 1, 2), mixed)
                    return 0

                lax.fori_loop(0, 6, face_a, 0)
                lax.fori_loop(1, 5, face_b, 0)

            def inner(t, _):
                for u in range(1, 5):
                    line(r, t * sa + u * sb, d, (0,) if boundary else (1, 2), mixed)
                return 0

            lax.fori_loop(1, 5, inner, 0)

    def settle():
        for d in range(3):
            sweep(T, d)

    loads[1].wait()
    loads[4].wait()
    drift = jnp.zeros((8, 128), F32)
    for c in range(8):
        drift = jnp.where(sub == c, drift_ref[c], drift)
    for d in range(3):
        pace = jnp.broadcast_to(motion_v[pl.ds(d, 1), :], (8, 128))
        if d == 2:
            pace = pace + drift
        consts[1 + d] = -STEP_LENGTH * pace

    loads[0].wait()

    def fetch(t, _):
        for k in range(6):
            n = t * 6 + k
            v = stage[pl.ds(n, 8, stride=NODES), :]
            T[n] = v * keep if k == 0 else v
        return 0

    lax.fori_loop(0, 36, fetch, 0)
    settle()
    pack(0)
    count = 1
    for axis, size in zip(AXES, sizes):
        here = lax.axis_index(axis)
        count = count * (1 + (here > 0).astype(jnp.int32) + (here < size - 1).astype(jnp.int32))
    pl.semaphore_wait(barrier, count - 1)
    start_all(0)

    def copy_over(t, _):
        for v in range(6):
            X[0, t * 6 + v] = T[t * 6 + v]
        return 0

    lax.fori_loop(0, 36, copy_over, 0)
    loads[2].wait()
    loads[3].wait()
    highest = lax.Precision.HIGHEST
    spread = (
        lax.broadcasted_iota(jnp.int32, (8, 256), 1) // 8 % 8
        == lax.broadcasted_iota(jnp.int32, (8, 256), 0)
    ).astype(F32)
    rows = []
    for a in range(8):
        block = rates_v[a]
        straight = jnp.dot(block, spread, precision=highest, preferred_element_type=F32)
        turned = lax.dot_general(
            block, spread, (((0,), (0,)), ((), ())), precision=highest, preferred_element_type=F32
        )
        rows.append(straight + turned)
    weights = STEP_LENGTH * jnp.concatenate(rows, axis=0)
    column = lax.broadcasted_iota(jnp.int32, (64, 256), 1)
    first = weights.astype(jnp.bfloat16).astype(F32)
    second = (weights - first).astype(jnp.bfloat16).astype(F32)
    third = (weights - first) - second
    parts = jnp.where(
        column < 64, first, jnp.where(column < 128, second, jnp.where(column < 192, third, 0.0))
    )
    for m in range(8):
        mix_lhs[pl.ds(64 * m, 64), :] = jnp.where(column % 8 == m, parts, 0.0).astype(jnp.bfloat16)

    for s in range(2):
        for b in range(8):
            state_f[s, b] = state_v[s, b].astype(F32)

    def contract(g, _):
        halves = []
        for s in range(2):
            block = state_f[s, :, pl.ds(pl.multiple_of(8 * g, 8), 8), :]
            halves.append(block.reshape(64, 128).astype(jnp.bfloat16))
        both = jnp.concatenate(halves, axis=1)
        stacked = jnp.concatenate([both] * 4, axis=0)
        res = jnp.dot(mix_lhs[...], stacked, preferred_element_type=F32)
        for s in range(2):
            mix[s, pl.ds(8 * g, 8)] = res[:, 128 * s : 128 * s + 128].reshape(8, 64, 128)
        return 0

    lax.fori_loop(0, 27, contract, 0)
    wait_sent(0)

    def section(r, _):
        wait_received(r)
        unpack(r)
        operator(r, True)
        settle()
        pack(r + 1)
        start_all(r + 1)
        operator(r, False)
        weight = r.astype(F32)

        def gather(t, _):
            for v in range(6):
                n = t * 6 + v
                X[r + 1, n] = X[0, n] + weight * X[r, n] + T[n]
            return 0

        lax.fori_loop(0, 36, gather, 0)
        wait_sent(r + 1)
        return 0

    lax.fori_loop(0, 2, section, 0)
    wait_received(2)
    unpack(2)

    def emit(t, _):
        for v in range(6):
            n = t * 6 + v
            out_ref[pl.ds(n, 8, stride=NODES), :] = 0.5 * X[2, n]
        return 0

    lax.fori_loop(0, 36, emit, 0)


def on_device(sizes, cost, states, rates, motion, drift, flags):
    elements = EX * EY * EZ
    hbm = pl.BlockSpec(memory_space=pltpu.HBM)
    operands = [
        pltpu.with_memory_space_constraint(x, pltpu.HBM)
        for x in (cost.reshape(8 * NODES, elements), states, rates, motion, drift, flags)
    ]
    tile = (8, 128)
    out = pl.pallas_call(
        functools.partial(kernel, sizes),
        out_shape=pltpu.VMEM((8 * NODES, elements), F32),
        in_specs=[hbm] * 6,
        out_specs=pl.BlockSpec(memory_space=pltpu.VMEM),
        scratch_shapes=[
            pltpu.SMEM((8,), F32),
            pltpu.SMEM((EX, EY), jnp.int32),
            pltpu.VMEM((8 * NODES, elements), F32),
            pltpu.VMEM((2, 8, NODES, elements), jnp.bfloat16),
            pltpu.VMEM((2, 8, NODES, elements), F32),
            pltpu.VMEM((8, 8, 8), F32),
            pltpu.VMEM((3, elements), F32),
            pltpu.VMEM((512, 256), jnp.bfloat16),
            pltpu.VMEM((2, NODES, 64, 128), F32),
            pltpu.VMEM((3, NODES) + tile, F32),
            pltpu.VMEM((NODES,) + tile, F32),
            pltpu.VMEM((4,) + tile, F32),
            pltpu.VMEM((3, SEND_TILES) + tile, F32),
            pltpu.VMEM((3, RECV_TILES) + tile, F32),
            pltpu.SemaphoreType.DMA((3, 26)),
            pltpu.SemaphoreType.DMA((3, 26)),
            pltpu.SemaphoreType.DMA((6,)),
        ],
        compiler_params=pltpu.CompilerParams(
            collective_id=0, has_side_effects=True, vmem_limit_bytes=52 << 20
        ),
        name="adjoint_sections",
    )(*operands)
    return out.reshape(8, NODES, elements)


def solution(mesh):
    sizes = tuple(mesh.shape[axis] for axis in AXES)
    in_specs = (
        P(None, None, AXES),
        P(None, None, None, AXES),
        P(),
        P(None, AXES),
        P(),
        P("gx", "gy"),
    )
    return jax.shard_map(
        functools.partial(on_device, sizes),
        mesh=mesh,
        in_specs=in_specs,
        out_specs=P(None, None, AXES),
        check_vma=False,
    )
```

```python
import functools

import jax
import jax.numpy as jnp
import numpy as np
from jax import lax
from jax.experimental import pallas as pl
from jax.experimental.pallas import tpu as pltpu
from jax.sharding import PartitionSpec as P

EX = 2
EY = 8
EZ = 8
STEP_LENGTH = 0.05
AXES = ("gx", "gy", "gz")
STRIDES = (36, 6, 1)
MESH = pl.DeviceIdType.MESH
NODES = 216
F32 = jnp.float32


def derivative_numbers():
    points = np.array(
        [-1.0, -0.765055323929465, -0.285231516480645, 0.285231516480645, 0.765055323929465, 1.0]
    )
    legendre = (63.0 * points**5 - 70.0 * points**3 + 15.0 * points) / 8.0
    matrix = np.zeros((6, 6))
    for row_index in range(6):
        for col_index in range(6):
            if row_index != col_index:
                matrix[row_index, col_index] = (
                    legendre[row_index]
                    / legendre[col_index]
                    / (points[row_index] - points[col_index])
                )
    matrix[0, 0] = -7.5
    matrix[5, 5] = 7.5
    return matrix


DMAT = derivative_numbers()
EVEN = [[0.5 * float(DMAT[i, m] + DMAT[5 - i, m]) for m in range(3)] for i in range(3)]
ODD = [[0.5 * float(DMAT[i, m] - DMAT[5 - i, m]) for m in range(3)] for i in range(3)]

INNER = [(a, b) for a in range(1, 5) for b in range(1, 5)]
Y_GROUPS = [
    [(0, k) for k in range(6)] + INNER[0:2],
    [(5, k) for k in range(6)] + INNER[2:4],
    [(i, 0) for i in range(6)] + INNER[4:6],
    [(i, 5) for i in range(6)] + INNER[6:8],
    INNER[8:16],
]
REST = [(i, j) for i in range(1, 5) for j in range(6)]
Z_GROUPS = [
    [(0, j) for j in range(6)] + REST[0:2],
    [(5, j) for j in range(6)] + REST[2:4],
    REST[4:12],
    REST[12:20],
    REST[20:24],
]
XL, XH, YL, YH, ZL, ZH, SEND_TILES = 0, 18, 36, 41, 46, 51, 56


def source_of(d):
    dx, dy, dz = d
    if dy == 0 and dz == 0:
        return (XL if dx < 0 else XH), 18
    if dx == 0 and dz == 0:
        return (YL if dy < 0 else YH), 5
    if dx == 0 and dy == 0:
        return (ZL if dz < 0 else ZH), 5
    if dy == 0:
        return (ZL if dz < 0 else ZH) + (0 if dx < 0 else 1), 1
    if dx != 0:
        return (YL if dy < 0 else YH) + (0 if dx < 0 else 1), 1
    return (YL if dy < 0 else YH) + (2 if dz < 0 else 3), 1


def directions():
    every = [(x, y, z) for x in (-1, 0, 1) for y in (-1, 0, 1) for z in (-1, 0, 1) if (x, y, z) != (0, 0, 0)]

    def rank(d):
        count = sum(abs(v) for v in d)
        if count == 3:
            return 0
        if count == 2:
            return 1 if d[1] == 0 else (2 if d[2] == 0 else 3)
        return 4 if d[2] else (5 if d[1] else 6)

    return sorted(every, key=rank)


DIRECTIONS = directions()
RECV_AT = {}
RECV_TILES = 0
for _d in DIRECTIONS:
    RECV_AT[_d] = RECV_TILES
    RECV_TILES += source_of(_d)[1]


def pieces():
    table = {n: [] for n in range(NODES)}
    for n in range(36):
        tile, shift = n % 18, (0 if n < 18 else 64)
        table[180 + n].append(((1, 0, 0), tile, shift, 0, 1))
        table[n].append(((-1, 0, 0), tile, shift, 0, 0))
    for g, group in enumerate(Y_GROUPS):
        for s, (i, k) in enumerate(group):
            table[i * 36 + 30 + k].append(((0, 1, 0), g, 8 * (7 - s), 1, 7))
            table[i * 36 + k].append(((0, -1, 0), g, -8 * s, 1, 0))
    for g, group in enumerate(Z_GROUPS):
        for s, (i, j) in enumerate(group):
            table[i * 36 + j * 6 + 5].append(((0, 0, 1), g, 7 - s, 2, 7))
            table[i * 36 + j * 6].append(((0, 0, -1), g, -s, 2, 0))
    return table


PIECES = pieces()
BOUNDARY = [n for n in range(NODES) if PIECES[n]]
INTERIOR = [n for n in range(NODES) if not PIECES[n]]


def roll(x, shift):
    shift = shift % 128
    return x if shift == 0 else pltpu.roll(x, shift, 1)


def exists(d, sizes):
    ok = None
    for axis, off, size in zip(AXES, d, sizes):
        if off == 0:
            continue
        here = lax.axis_index(axis)
        term = here < size - 1 if off > 0 else here > 0
        ok = term if ok is None else jnp.logical_and(ok, term)
    return ok


def device_at(d):
    return {axis: lax.axis_index(axis) + off for axis, off in zip(AXES, d) if off != 0}


def kernel(
    sizes, cost_hbm, state_hbm, rates_hbm, motion_hbm, drift_hbm, flags_hbm, out_ref,
    drift_ref, flags_ref, stage, state_v, state_f, rates_v, motion_v, mix_lhs, mix, X, T, consts,
    send_buf, recv_buf, send_sem, recv_sem, load_sem,
):
    lane = lax.broadcasted_iota(jnp.int32, (8, 128), 1)
    sub = lax.broadcasted_iota(jnp.int32, (8, 128), 0)
    p_at, q_at, r_at = lane // 64, (lane // 8) % 8, lane % 8

    loads = [
        pltpu.make_async_copy(cost_hbm, stage, load_sem.at[0]),
        pltpu.make_async_copy(motion_hbm, motion_v, load_sem.at[1]),
        pltpu.make_async_copy(rates_hbm, rates_v, load_sem.at[2]),
        pltpu.make_async_copy(state_hbm, state_v, load_sem.at[3]),
        pltpu.make_async_copy(drift_hbm, drift_ref, load_sem.at[4]),
        pltpu.make_async_copy(flags_hbm, flags_ref, load_sem.at[5]),
    ]
    for load in loads:
        load.start()

    barrier = pltpu.get_barrier_semaphore()
    for d in DIRECTIONS:
        @pl.when(exists(d, sizes))
        def _():
            pl.semaphore_signal(barrier, inc=1, device_id=device_at(d), device_id_type=MESH)

    for d in DIRECTIONS:
        n = source_of(d)[1]

        @pl.when(jnp.logical_not(exists(tuple(-v for v in d), sizes)))
        def _():
            for s in range(3):
                recv_buf[s, pl.ds(RECV_AT[d], n)] = jnp.zeros((n, 8, 128), F32)

    loads[5].wait()
    keep = jnp.ones((8, 128), F32)
    bottom = lax.axis_index("gz") == 0
    for p in range(EX):
        for q in range(EY):
            open_here = 1.0 - flags_ref[p, q].astype(F32)
            hit = jnp.logical_and(lane == p * 64 + q * 8, bottom)
            keep = jnp.where(hit, open_here, keep)
    consts[0] = keep

    def sweep(ref, d):
        a_d, b_d = [x for x in range(3) if x != d]
        shift = (64, 8, 1)[d]
        at = (p_at, q_at, r_at)[d]
        last = (1, 7, 7)[d]

        for t in range(6):
            for u in range(6):
                lo_n = t * STRIDES[a_d] + u * STRIDES[b_d]
                hi_n = lo_n + 5 * STRIDES[d]
                a, b = ref[lo_n], ref[hi_n]
                if d == 0:
                    both = jnp.where(at == 1, a, b)
                    both = both + roll(both, 64)
                    ref[lo_n] = jnp.where(at == 1, both, a)
                    ref[hi_n] = jnp.where(at == 0, both, b)
                else:
                    s = a + roll(b, shift)
                    ref[lo_n] = jnp.where(at > 0, s, a)
                    ref[hi_n] = jnp.where(at < last, roll(s, -shift), b)

    def pack(slot):
        for g, group in enumerate(Y_GROUPS):
            low = high = jnp.zeros((8, 128), F32)
            for s, (i, k) in enumerate(group):
                low = jnp.where(q_at == s, roll(T[i * 36 + k], 8 * s), low)
                high = jnp.where(q_at == s, roll(T[i * 36 + 30 + k], 8 * (s - 7)), high)
            send_buf[slot, YL + g] = low
            send_buf[slot, YH + g] = high
        for g, group in enumerate(Z_GROUPS):
            low = high = jnp.zeros((8, 128), F32)
            for s, (i, j) in enumerate(group):
                low = jnp.where(r_at == s, roll(T[i * 36 + j * 6], s), low)
                high = jnp.where(r_at == s, roll(T[i * 36 + j * 6 + 5], s - 7), high)
            send_buf[slot, ZL + g] = low
            send_buf[slot, ZH + g] = high

        def body(t, _):
            for v in range(6):
                n = t * 6 + v
                send_buf[slot, XL + n] = jnp.where(p_at == 1, roll(T[n], 64), T[n + 18])
                send_buf[slot, XH + n] = jnp.where(p_at == 0, roll(T[180 + n], 64), T[180 + n + 18])
            return 0

        lax.fori_loop(0, 3, body, 0)

    def message(slot, m):
        d = DIRECTIONS[m]
        at, n = source_of(d)
        return pltpu.make_async_remote_copy(
            src_ref=send_buf.at[slot, pl.ds(at, n)],
            dst_ref=recv_buf.at[slot, pl.ds(RECV_AT[d], n)],
            send_sem=send_sem.at[slot, m],
            recv_sem=recv_sem.at[slot, m],
            device_id=device_at(d),
            device_id_type=MESH,
        )

    def start_all(slot):
        for m, d in enumerate(DIRECTIONS):
            @pl.when(exists(d, sizes))
            def _():
                message(slot, m).start()

    def wait_sent(slot):
        for m, d in enumerate(DIRECTIONS):
            @pl.when(exists(d, sizes))
            def _():
                message(slot, m).wait_send()

    def wait_received(slot):
        for m, d in enumerate(DIRECTIONS):
            @pl.when(exists(tuple(-v for v in d), sizes))
            def _():
                message(slot, m).wait_recv()

    def got(slot, f, tile=0):
        return recv_buf[slot, RECV_AT[tuple(-v for v in f)] + tile]

    def join(slot):
        zero = jnp.zeros((8, 128), F32)
        for fy in (1, -1):
            for g in range(4):
                v = got(slot, (0, fy, 0), g)
                if g < 2:
                    fx = 1 if g == 1 else -1
                    mine = jnp.logical_and(p_at == (1 if fx > 0 else 0), q_at < 6)
                    v = v + jnp.where(mine, roll(got(slot, (fx, fy, 0)), 64), zero)
                    for fz in (1, -1):
                        target = (64 if fx > 0 else 0) + (47 if fz > 0 else 0)
                        origin = (0 if fx > 0 else 64) + (0 if fz > 0 else 47)
                        v = v + jnp.where(lane == target, roll(got(slot, (fx, fy, fz)), target - origin), zero)
                else:
                    fz = 1 if g == 3 else -1
                    v = jnp.where(jnp.logical_or(q_at == 0, q_at == 5), zero, v)
                    mine = jnp.logical_and(r_at == (7 if fz > 0 else 0), q_at < 6)
                    v = v + jnp.where(mine, roll(got(slot, (0, fy, fz)), 7 * fz), zero)
                recv_buf[slot, RECV_AT[(0, -fy, 0)] + g] = v
        for fz in (1, -1):
            for g in range(2):
                fx = 1 if g == 1 else -1
                mine = jnp.logical_and(p_at == (1 if fx > 0 else 0), r_at < 6)
                v = got(slot, (0, 0, fz), g) + jnp.where(mine, roll(got(slot, (fx, 0, fz)), 64), zero)
                recv_buf[slot, RECV_AT[(0, 0, -fz)] + g] = v

    masks = {0: p_at, 1: q_at, 2: r_at}

    def unpack(slot, put):
        join(slot)
        zero = jnp.zeros((8, 128), F32)
        for n in BOUNDARY:
            value = X[slot, n]
            for f, tile, shift, d, place in PIECES[n]:
                value = value + jnp.where(masks[d] == place, roll(got(slot, f, tile), shift), zero)
            put(n, value)

    def line(r, base, d, outputs, with_mix):
        stride = STRIDES[d]
        h = [X[r, base + m * stride] for m in range(6)]
        even = [h[i] + h[5 - i] for i in range(3)]
        odd = [h[i] - h[5 - i] for i in range(3)]
        speed = consts[1 + d]
        for m in range(3):
            if m not in outputs:
                continue
            pe = EVEN[0][m] * even[0] + EVEN[1][m] * even[1] + EVEN[2][m] * even[2]
            qo = ODD[0][m] * odd[0] + ODD[1][m] * odd[1] + ODD[2][m] * odd[2]
            for at, value in ((m, qo + pe), (5 - m, qo - pe)):
                n = base + at * stride
                value = speed * value
                if d > 0:
                    value = value + T[n]
                if with_mix:
                    for a in range(8):
                        value = value + mix[1 - r, n, pl.ds(8 * a, 8), :] * X[r, n, pl.ds(a, 1), :]
                    if at == 0:
                        value = value * consts[0]
                T[n] = value

    def operator(r, boundary):
        for d in range(3):
            a_d, b_d = [x for x in range(3) if x != d]
            sa, sb = STRIDES[a_d], STRIDES[b_d]
            mixed = d == 2
            for t in range(6):
                for u in range(6):
                    whole = t in (0, 5) or u in (0, 5)
                    if boundary:
                        line(r, t * sa + u * sb, d, (0, 1, 2) if whole else (0,), mixed)
                    elif not whole:
                        line(r, t * sa + u * sb, d, (1, 2), mixed)

    def settle():
        for d in range(3):
            sweep(T, d)

    loads[1].wait()
    loads[4].wait()
    drift = jnp.zeros((8, 128), F32)
    for c in range(8):
        drift = jnp.where(sub == c, drift_ref[c], drift)
    for d in range(3):
        pace = jnp.broadcast_to(motion_v[pl.ds(d, 1), :], (8, 128))
        if d == 2:
            pace = pace + drift
        consts[1 + d] = -STEP_LENGTH * pace

    loads[0].wait()

    def fetch(t, _):
        for k in range(36):
            n = t * 36 + k
            v = stage[pl.ds(n, 8, stride=NODES), :]
            T[n] = v * keep if k % 6 == 0 else v
        return 0

    lax.fori_loop(0, 6, fetch, 0)
    settle()
    pack(0)
    count = 1
    for axis, size in zip(AXES, sizes):
        here = lax.axis_index(axis)
        count = count * (1 + (here > 0).astype(jnp.int32) + (here < size - 1).astype(jnp.int32))
    pl.semaphore_wait(barrier, count - 1)
    start_all(0)

    def copy_over(t, _):
        for v in range(24):
            X[0, t * 24 + v] = T[t * 24 + v]
        return 0

    lax.fori_loop(0, 9, copy_over, 0)
    loads[2].wait()
    loads[3].wait()
    highest = lax.Precision.HIGHEST
    spread = (
        lax.broadcasted_iota(jnp.int32, (8, 256), 1) // 8 % 8
        == lax.broadcasted_iota(jnp.int32, (8, 256), 0)
    ).astype(F32)
    rows = []
    for a in range(8):
        block = rates_v[a]
        straight = jnp.dot(block, spread, precision=highest, preferred_element_type=F32)
        turned = lax.dot_general(
            block, spread, (((0,), (0,)), ((), ())), precision=highest, preferred_element_type=F32
        )
        rows.append(straight + turned)
    weights = STEP_LENGTH * jnp.concatenate(rows, axis=0)
    column = lax.broadcasted_iota(jnp.int32, (64, 256), 1)
    first = weights.astype(jnp.bfloat16).astype(F32)
    second = (weights - first).astype(jnp.bfloat16).astype(F32)
    third = (weights - first) - second
    parts = jnp.where(
        column < 64, first, jnp.where(column < 128, second, jnp.where(column < 192, third, 0.0))
    )
    for m in range(8):
        mix_lhs[pl.ds(64 * m, 64), :] = jnp.where(column % 8 == m, parts, 0.0).astype(jnp.bfloat16)

    def contract(s):
        for b in range(8):
            state_f[b, pl.ds(0, NODES)] = state_v[s, b].astype(F32)

        def body(g, _):
            base = pl.multiple_of(16 * g, 16)
            halves = []
            for half in range(2):
                block = state_f[:, pl.ds(base + 8 * half, 8), :]
                halves.append(block.reshape(64, 128).astype(jnp.bfloat16))
            both = jnp.concatenate(halves, axis=1)
            stacked = jnp.concatenate([both] * 4, axis=0)
            res = jnp.dot(mix_lhs[...], stacked, preferred_element_type=F32)
            for half in range(2):
                mix[s, pl.ds(base + 8 * half, 8)] = res[:, 128 * half : 128 * half + 128].reshape(8, 64, 128)
            return 0

        lax.fori_loop(0, 14, body, 0)

    state_f[:, pl.ds(NODES, 8), :] = jnp.zeros((8, 8, 128), F32)
    contract(1)
    wait_sent(0)

    def section(r, _):
        wait_received(r)

        def keep_value(n, value):
            X[r, n] = value

        unpack(r, keep_value)
        operator(r, True)
        settle()
        pack(r + 1)
        start_all(r + 1)
        operator(r, False)
        weight = r.astype(F32)

        def gather(t, _):
            for v in range(24):
                n = t * 24 + v
                X[r + 1, n] = X[0, n] + weight * X[r, n] + T[n]
            return 0

        lax.fori_loop(0, 9, gather, 0)

        @pl.when(r == 0)
        def _():
            contract(0)

        wait_sent(r + 1)
        return 0

    lax.fori_loop(0, 2, section, 0)

    def emit(n, value):
        out_ref[pl.ds(n, 8, stride=NODES), :] = 0.5 * value

    for n in INTERIOR:
        emit(n, X[2, n])
    wait_received(2)
    unpack(2, emit)


def on_device(sizes, cost, states, rates, motion, drift, flags):
    elements = EX * EY * EZ
    hbm = pl.BlockSpec(memory_space=pltpu.HBM)
    operands = [
        pltpu.with_memory_space_constraint(x, pltpu.HBM)
        for x in (cost.reshape(8 * NODES, elements), states, rates, motion, drift, flags)
    ]
    tile = (8, 128)
    out = pl.pallas_call(
        functools.partial(kernel, sizes),
        out_shape=pltpu.VMEM((8 * NODES, elements), F32),
        in_specs=[hbm] * 6,
        out_specs=pl.BlockSpec(memory_space=pltpu.VMEM),
        scratch_shapes=[
            pltpu.SMEM((8,), F32),
            pltpu.SMEM((EX, EY), jnp.int32),
            pltpu.VMEM((8 * NODES, elements), F32),
            pltpu.VMEM((2, 8, NODES, elements), jnp.bfloat16),
            pltpu.VMEM((8, NODES + 8, elements), F32),
            pltpu.VMEM((8, 8, 8), F32),
            pltpu.VMEM((3, elements), F32),
            pltpu.VMEM((512, 256), jnp.bfloat16),
            pltpu.VMEM((2, NODES + 8, 64, 128), F32),
            pltpu.VMEM((3, NODES) + tile, F32),
            pltpu.VMEM((NODES,) + tile, F32),
            pltpu.VMEM((4,) + tile, F32),
            pltpu.VMEM((3, SEND_TILES) + tile, F32),
            pltpu.VMEM((3, RECV_TILES) + tile, F32),
            pltpu.SemaphoreType.DMA((3, 26)),
            pltpu.SemaphoreType.DMA((3, 26)),
            pltpu.SemaphoreType.DMA((6,)),
        ],
        compiler_params=pltpu.CompilerParams(
            collective_id=0, has_side_effects=True, vmem_limit_bytes=52 << 20
        ),
        name="adjoint_sections",
    )(*operands)
    return out.reshape(8, NODES, elements)


def solution(mesh):
    sizes = tuple(mesh.shape[axis] for axis in AXES)
    in_specs = (
        P(None, None, AXES),
        P(None, None, None, AXES),
        P(),
        P(None, AXES),
        P(),
        P("gx", "gy"),
    )
    return jax.shard_map(
        functools.partial(on_device, sizes),
        mesh=mesh,
        in_specs=in_specs,
        out_specs=P(None, None, AXES),
        check_vma=False,
    )
```

```python
import functools

import jax
import jax.numpy as jnp
import numpy as np
from jax import lax
from jax.experimental import pallas as pl
from jax.experimental.pallas import tpu as pltpu
from jax.sharding import PartitionSpec as P

EX = 2
EY = 8
EZ = 8
STEP_LENGTH = 0.05
AXES = ("gx", "gy", "gz")
STRIDES = (36, 6, 1)
MESH = pl.DeviceIdType.MESH
NODES = 216
F32 = jnp.float32


def derivative_numbers():
    points = np.array(
        [-1.0, -0.765055323929465, -0.285231516480645, 0.285231516480645, 0.765055323929465, 1.0]
    )
    legendre = (63.0 * points**5 - 70.0 * points**3 + 15.0 * points) / 8.0
    matrix = np.zeros((6, 6))
    for row_index in range(6):
        for col_index in range(6):
            if row_index != col_index:
                matrix[row_index, col_index] = (
                    legendre[row_index]
                    / legendre[col_index]
                    / (points[row_index] - points[col_index])
                )
    matrix[0, 0] = -7.5
    matrix[5, 5] = 7.5
    return matrix


DMAT = derivative_numbers()
EVEN = [[0.5 * float(DMAT[i, m] + DMAT[5 - i, m]) for m in range(3)] for i in range(3)]
ODD = [[0.5 * float(DMAT[i, m] - DMAT[5 - i, m]) for m in range(3)] for i in range(3)]

INNER = [(a, b) for a in range(1, 5) for b in range(1, 5)]
Y_GROUPS = [
    [(0, k) for k in range(6)] + INNER[0:2],
    [(5, k) for k in range(6)] + INNER[2:4],
    [(i, 0) for i in range(6)] + INNER[4:6],
    [(i, 5) for i in range(6)] + INNER[6:8],
    INNER[8:16],
]
REST = [(i, j) for i in range(1, 5) for j in range(6)]
Z_GROUPS = [
    [(0, j) for j in range(6)] + REST[0:2],
    [(5, j) for j in range(6)] + REST[2:4],
    REST[4:12],
    REST[12:20],
    REST[20:24],
]
X_HALVES = [(j, k) for j in range(5) for k in range(5)] + ["depth", "height", None]
X_TILES = 14
XL, XH, YL, YH, ZL, ZH, SEND_TILES = 0, 14, 28, 33, 38, 43, 48


def source_of(d):
    dx, dy, dz = d
    if dy == 0 and dz == 0:
        return (XL if dx < 0 else XH), X_TILES
    if dx == 0 and dz == 0:
        return (YL if dy < 0 else YH), 5
    if dx == 0 and dy == 0:
        return (ZL if dz < 0 else ZH), 5
    return (YL if dy < 0 else YH) + (2 if dz < 0 else 3), 1


def half_source_of(d):
    dx, dy, dz = d
    side = 0 if dx < 0 else 1
    if dy == 0:
        return 4 + 2 * (dz > 0) + side, (ZL if dz < 0 else ZH) + side
    return 2 * (dy > 0) + side, (YL if dy < 0 else YH) + side


def is_half(d):
    return d[0] != 0 and (d[1] != 0 or d[2] != 0)


def directions():
    every = [(x, y, z) for x in (-1, 0, 1) for y in (-1, 0, 1) for z in (-1, 0, 1) if (x, y, z) != (0, 0, 0)]

    def rank(d):
        count = sum(abs(v) for v in d)
        if count == 3:
            return 0
        if count == 2:
            return 1 if d[1] == 0 else (2 if d[2] == 0 else 3)
        return 4 if d[2] else (5 if d[1] else 6)

    return sorted(every, key=rank)


DIRECTIONS = directions()
RECV_AT = {}
RECV_TILES = 0
HALF_AT = {}
for _d in DIRECTIONS:
    if is_half(_d):
        HALF_AT[_d] = len(HALF_AT)
    else:
        RECV_AT[_d] = RECV_TILES
        RECV_TILES += source_of(_d)[1]


def pieces():
    table = {n: [] for n in range(NODES)}
    where = {h: (x // 2, 64 * (x % 2)) for x, h in enumerate(X_HALVES)}
    for f, base, p in ((1, 180, 1), (-1, 0, 0)):
        def add(j, k, half, shift, q, r):
            tile, across = where[half]
            table[base + j * 6 + k].append(((f, 0, 0), tile, across + shift, (p, q, r)))

        for j in range(5):
            for k in range(5):
                add(j, k, (j, k), 0, None, None)
        for t in range(5):
            add(5, t, (0, t), -8, "below", None)
            add(5, t, "depth", 8 * (7 - t), 7, None)
            add(t, 5, (t, 0), -1, None, "below")
            add(t, 5, "height", 7 - t, None, 7)
        add(5, 5, (0, 0), -9, "below", "below")
        add(5, 5, "depth", 8 * (7 - 5), 7, None)
        add(5, 5, "height", 7 - 8, "below", 7)
    for g, group in enumerate(Y_GROUPS):
        for s, (i, k) in enumerate(group):
            table[i * 36 + 30 + k].append(((0, 1, 0), g, 8 * (7 - s), (None, 7, None)))
            table[i * 36 + k].append(((0, -1, 0), g, -8 * s, (None, 0, None)))
    for g, group in enumerate(Z_GROUPS):
        for s, (i, j) in enumerate(group):
            table[i * 36 + j * 6 + 5].append(((0, 0, 1), g, 7 - s, (None, None, 7)))
            table[i * 36 + j * 6].append(((0, 0, -1), g, -s, (None, None, 0)))
    return table


HALF_FROM = dict(half_source_of(d) for d in DIRECTIONS if is_half(d))
PIECES = pieces()
BOUNDARY = [n for n in range(NODES) if PIECES[n]]
INTERIOR = [n for n in range(NODES) if not PIECES[n]]


def roll(x, shift):
    shift = shift % 128
    return x if shift == 0 else pltpu.roll(x, shift, 1)


def exists(d, sizes):
    ok = None
    for axis, off, size in zip(AXES, d, sizes):
        if off == 0:
            continue
        here = lax.axis_index(axis)
        term = here < size - 1 if off > 0 else here > 0
        ok = term if ok is None else jnp.logical_and(ok, term)
    return ok


def device_at(d):
    return {axis: lax.axis_index(axis) + off for axis, off in zip(AXES, d) if off != 0}


def kernel(
    sizes, cost_hbm, state_hbm, rates_hbm, motion_hbm, drift_hbm, flags_hbm, out_ref,
    drift_ref, flags_ref, stage, state_v, state_f, rates_v, motion_v, mix_lhs, mix, X, T, consts,
    send_buf, recv_buf, send_half, recv_half, send_sem, recv_sem, load_sem,
):
    lane = lax.broadcasted_iota(jnp.int32, (8, 128), 1)
    sub = lax.broadcasted_iota(jnp.int32, (8, 128), 0)
    p_at, q_at, r_at = lane // 64, (lane // 8) % 8, lane % 8

    loads = [
        pltpu.make_async_copy(cost_hbm, stage, load_sem.at[0]),
        pltpu.make_async_copy(motion_hbm, motion_v, load_sem.at[1]),
        pltpu.make_async_copy(rates_hbm, rates_v, load_sem.at[2]),
        pltpu.make_async_copy(state_hbm, state_v, load_sem.at[3]),
        pltpu.make_async_copy(drift_hbm, drift_ref, load_sem.at[4]),
        pltpu.make_async_copy(flags_hbm, flags_ref, load_sem.at[5]),
    ]
    for load in loads:
        load.start()

    barrier = pltpu.get_barrier_semaphore()
    for d in DIRECTIONS:
        @pl.when(exists(d, sizes))
        def _():
            pl.semaphore_signal(barrier, inc=1, device_id=device_at(d), device_id_type=MESH)

    for d in DIRECTIONS:
        @pl.when(jnp.logical_not(exists(tuple(-v for v in d), sizes)))
        def _():
            for s in range(3):
                if is_half(d):
                    recv_half[s, HALF_AT[d]] = jnp.zeros((4, 128), F32)
                else:
                    n = source_of(d)[1]
                    recv_buf[s, pl.ds(RECV_AT[d], n)] = jnp.zeros((n, 8, 128), F32)

    loads[5].wait()
    keep = jnp.ones((8, 128), F32)
    bottom = lax.axis_index("gz") == 0
    for p in range(EX):
        for q in range(EY):
            open_here = 1.0 - flags_ref[p, q].astype(F32)
            hit = jnp.logical_and(lane == p * 64 + q * 8, bottom)
            keep = jnp.where(hit, open_here, keep)
    consts[0] = keep

    def sweep(ref, d):
        a_d, b_d = [x for x in range(3) if x != d]
        shift = (64, 8, 1)[d]
        at = (p_at, q_at, r_at)[d]
        last = (1, 7, 7)[d]

        for t in range(6):
            for u in range(6):
                lo_n = t * STRIDES[a_d] + u * STRIDES[b_d]
                hi_n = lo_n + 5 * STRIDES[d]
                a, b = ref[lo_n], ref[hi_n]
                if d == 0:
                    both = jnp.where(at == 1, a, b)
                    both = both + roll(both, 64)
                    ref[lo_n] = jnp.where(at == 1, both, a)
                    ref[hi_n] = jnp.where(at == 0, both, b)
                else:
                    s = a + roll(b, shift)
                    ref[lo_n] = jnp.where(at > 0, s, a)
                    ref[hi_n] = jnp.where(at < last, roll(s, -shift), b)

    def pack(slot):
        for g, group in enumerate(Y_GROUPS):
            low = high = jnp.zeros((8, 128), F32)
            for s, (i, k) in enumerate(group):
                low = jnp.where(q_at == s, roll(T[i * 36 + k], 8 * s), low)
                high = jnp.where(q_at == s, roll(T[i * 36 + 30 + k], 8 * (s - 7)), high)
            send_buf[slot, YL + g] = low
            send_buf[slot, YH + g] = high
        for g, group in enumerate(Z_GROUPS):
            low = high = jnp.zeros((8, 128), F32)
            for s, (i, j) in enumerate(group):
                low = jnp.where(r_at == s, roll(T[i * 36 + j * 6], s), low)
                high = jnp.where(r_at == s, roll(T[i * 36 + j * 6 + 5], s - 7), high)
            send_buf[slot, ZL + g] = low
            send_buf[slot, ZH + g] = high

        for at in range(8):
            full = send_buf[slot, HALF_FROM[at]]
            other = roll(pltpu.roll(full, 4, 0), 64)
            send_half[slot, at] = jnp.where(p_at == at % 2, full, other)[0:4]

        def half(h, high):
            if h == "depth":
                return send_buf[slot, YH + high]
            if h == "height":
                return send_buf[slot, ZH + high]
            return T[180 * high + h[0] * 6 + h[1]]

        for t in range(X_TILES):
            for high, at in ((0, XL), (1, XH)):
                tile = roll(half(X_HALVES[2 * t], high), 64)
                if X_HALVES[2 * t + 1] is not None:
                    tile = jnp.where(p_at == 1 - high, tile, half(X_HALVES[2 * t + 1], high))
                send_buf[slot, at + t] = tile

    def message(slot, m):
        d = DIRECTIONS[m]
        if is_half(d):
            src = send_half.at[slot, half_source_of(d)[0]]
            dst = recv_half.at[slot, HALF_AT[d]]
        else:
            at, n = source_of(d)
            src = send_buf.at[slot, pl.ds(at, n)]
            dst = recv_buf.at[slot, pl.ds(RECV_AT[d], n)]
        return pltpu.make_async_remote_copy(
            src_ref=src,
            dst_ref=dst,
            send_sem=send_sem.at[slot, m],
            recv_sem=recv_sem.at[slot, m],
            device_id=device_at(d),
            device_id_type=MESH,
        )

    def start_all(slot):
        for m, d in enumerate(DIRECTIONS):
            @pl.when(exists(d, sizes))
            def _():
                message(slot, m).start()

    def wait_sent(slot):
        for m, d in enumerate(DIRECTIONS):
            @pl.when(exists(d, sizes))
            def _():
                message(slot, m).wait_send()

    def wait_received(slot):
        for m, d in enumerate(DIRECTIONS):
            @pl.when(exists(tuple(-v for v in d), sizes))
            def _():
                message(slot, m).wait_recv()

    def got(slot, f, tile=0):
        return recv_buf[slot, RECV_AT[tuple(-v for v in f)] + tile]

    def got_half(slot, f):
        part = recv_half[slot, HALF_AT[tuple(-v for v in f)]]
        return jnp.concatenate([roll(part, 64), part], axis=0)

    def join(slot):
        zero = jnp.zeros((8, 128), F32)
        for fy in (1, -1):
            for g in range(4):
                v = got(slot, (0, fy, 0), g)
                if g < 2:
                    fx = 1 if g == 1 else -1
                    mine = jnp.logical_and(p_at == (1 if fx > 0 else 0), q_at < 6)
                    v = v + jnp.where(mine, got_half(slot, (fx, fy, 0)), zero)
                    for fz in (1, -1):
                        target = (64 if fx > 0 else 0) + (47 if fz > 0 else 0)
                        origin = (0 if fx > 0 else 64) + (0 if fz > 0 else 47)
                        v = v + jnp.where(lane == target, roll(got_half(slot, (fx, fy, fz)), target - origin - 64), zero)
                else:
                    fz = 1 if g == 3 else -1
                    v = jnp.where(jnp.logical_or(q_at == 0, q_at == 5), zero, v)
                    mine = jnp.logical_and(r_at == (7 if fz > 0 else 0), q_at < 6)
                    v = v + jnp.where(mine, roll(got(slot, (0, fy, fz)), 7 * fz), zero)
                recv_buf[slot, RECV_AT[(0, -fy, 0)] + g] = v
        for fz in (1, -1):
            for g in range(2):
                fx = 1 if g == 1 else -1
                mine = jnp.logical_and(p_at == (1 if fx > 0 else 0), r_at < 6)
                v = got(slot, (0, 0, fz), g) + jnp.where(mine, got_half(slot, (fx, 0, fz)), zero)
                recv_buf[slot, RECV_AT[(0, 0, -fz)] + g] = v

    def masked(places):
        mask = None
        for at, place in zip((p_at, q_at, r_at), places):
            if place is not None:
                term = at < 7 if place == "below" else at == place
                mask = term if mask is None else jnp.logical_and(mask, term)
        return mask

    def unpack(slot, put):
        join(slot)
        zero = jnp.zeros((8, 128), F32)
        for n in BOUNDARY:
            value = X[slot, n]
            for f, tile, shift, places in PIECES[n]:
                value = value + jnp.where(masked(places), roll(got(slot, f, tile), shift), zero)
            put(n, value)

    def line(r, base, d, outputs, with_mix):
        stride = STRIDES[d]
        h = [X[r, base + m * stride] for m in range(6)]
        even = [h[i] + h[5 - i] for i in range(3)]
        odd = [h[i] - h[5 - i] for i in range(3)]
        speed = consts[1 + d]
        for m in range(3):
            if m not in outputs:
                continue
            pe = EVEN[0][m] * even[0] + EVEN[1][m] * even[1] + EVEN[2][m] * even[2]
            qo = ODD[0][m] * odd[0] + ODD[1][m] * odd[1] + ODD[2][m] * odd[2]
            for at, value in ((m, qo + pe), (5 - m, qo - pe)):
                n = base + at * stride
                value = speed * value
                if d > 0:
                    value = value + T[n]
                if with_mix:
                    for a in range(8):
                        value = value + mix[1 - r, n, pl.ds(8 * a, 8), :] * X[r, n, pl.ds(a, 1), :]
                    if at == 0:
                        value = value * consts[0]
                T[n] = value

    def operator(r, boundary):
        for d in range(3):
            a_d, b_d = [x for x in range(3) if x != d]
            sa, sb = STRIDES[a_d], STRIDES[b_d]
            mixed = d == 2
            for t in range(6):
                for u in range(6):
                    whole = t in (0, 5) or u in (0, 5)
                    if boundary:
                        line(r, t * sa + u * sb, d, (0, 1, 2) if whole else (0,), mixed)
                    elif not whole:
                        line(r, t * sa + u * sb, d, (1, 2), mixed)

    def settle():
        for d in range(3):
            sweep(T, d)

    loads[1].wait()
    loads[4].wait()
    drift = jnp.zeros((8, 128), F32)
    for c in range(8):
        drift = jnp.where(sub == c, drift_ref[c], drift)
    for d in range(3):
        pace = jnp.broadcast_to(motion_v[pl.ds(d, 1), :], (8, 128))
        if d == 2:
            pace = pace + drift
        consts[1 + d] = -STEP_LENGTH * pace

    loads[0].wait()

    def fetch(t, _):
        for k in range(36):
            n = t * 36 + k
            v = stage[pl.ds(n, 8, stride=NODES), :]
            T[n] = v * keep if k % 6 == 0 else v
        return 0

    lax.fori_loop(0, 6, fetch, 0)
    settle()
    pack(0)
    count = 1
    for axis, size in zip(AXES, sizes):
        here = lax.axis_index(axis)
        count = count * (1 + (here > 0).astype(jnp.int32) + (here < size - 1).astype(jnp.int32))
    pl.semaphore_wait(barrier, count - 1)
    start_all(0)

    def copy_over(t, _):
        for v in range(24):
            X[0, t * 24 + v] = T[t * 24 + v]
        return 0

    lax.fori_loop(0, 9, copy_over, 0)
    loads[2].wait()
    loads[3].wait()
    highest = lax.Precision.HIGHEST
    spread = (
        lax.broadcasted_iota(jnp.int32, (8, 256), 1) // 8 % 8
        == lax.broadcasted_iota(jnp.int32, (8, 256), 0)
    ).astype(F32)
    rows = []
    for a in range(8):
        block = rates_v[a]
        straight = jnp.dot(block, spread, precision=highest, preferred_element_type=F32)
        turned = lax.dot_general(
            block, spread, (((0,), (0,)), ((), ())), precision=highest, preferred_element_type=F32
        )
        rows.append(straight + turned)
    weights = STEP_LENGTH * jnp.concatenate(rows, axis=0)
    column = lax.broadcasted_iota(jnp.int32, (64, 256), 1)
    first = weights.astype(jnp.bfloat16).astype(F32)
    second = (weights - first).astype(jnp.bfloat16).astype(F32)
    third = (weights - first) - second
    parts = jnp.where(
        column < 64, first, jnp.where(column < 128, second, jnp.where(column < 192, third, 0.0))
    )
    for m in range(8):
        mix_lhs[pl.ds(64 * m, 64), :] = jnp.where(column % 8 == m, parts, 0.0).astype(jnp.bfloat16)

    def contract(s):
        for b in range(8):
            state_f[b, pl.ds(0, NODES)] = state_v[s, b].astype(F32)

        def body(g, _):
            base = pl.multiple_of(16 * g, 16)
            halves = []
            for half in range(2):
                block = state_f[:, pl.ds(base + 8 * half, 8), :]
                halves.append(block.reshape(64, 128).astype(jnp.bfloat16))
            both = jnp.concatenate(halves, axis=1)
            stacked = jnp.concatenate([both] * 4, axis=0)
            res = jnp.dot(mix_lhs[...], stacked, preferred_element_type=F32)
            for half in range(2):
                mix[s, pl.ds(base + 8 * half, 8)] = res[:, 128 * half : 128 * half + 128].reshape(8, 64, 128)
            return 0

        lax.fori_loop(0, 14, body, 0)

    state_f[:, pl.ds(NODES, 8), :] = jnp.zeros((8, 8, 128), F32)
    contract(1)
    wait_sent(0)

    def section(r, _):
        wait_received(r)

        def keep_value(n, value):
            X[r, n] = value

        unpack(r, keep_value)
        operator(r, True)
        settle()
        pack(r + 1)
        start_all(r + 1)
        operator(r, False)
        weight = r.astype(F32)

        def gather(t, _):
            for v in range(24):
                n = t * 24 + v
                X[r + 1, n] = X[0, n] + weight * X[r, n] + T[n]
            return 0

        lax.fori_loop(0, 9, gather, 0)

        @pl.when(r == 0)
        def _():
            contract(0)

        wait_sent(r + 1)
        return 0

    lax.fori_loop(0, 2, section, 0)

    def emit(n, value):
        out_ref[pl.ds(n, 8, stride=NODES), :] = 0.5 * value

    for n in INTERIOR:
        emit(n, X[2, n])
    wait_received(2)
    unpack(2, emit)


def on_device(sizes, cost, states, rates, motion, drift, flags):
    elements = EX * EY * EZ
    hbm = pl.BlockSpec(memory_space=pltpu.HBM)
    operands = [
        pltpu.with_memory_space_constraint(x, pltpu.HBM)
        for x in (cost.reshape(8 * NODES, elements), states, rates, motion, drift, flags)
    ]
    tile = (8, 128)
    out = pl.pallas_call(
        functools.partial(kernel, sizes),
        out_shape=pltpu.VMEM((8 * NODES, elements), F32),
        in_specs=[hbm] * 6,
        out_specs=pl.BlockSpec(memory_space=pltpu.VMEM),
        scratch_shapes=[
            pltpu.SMEM((8,), F32),
            pltpu.SMEM((EX, EY), jnp.int32),
            pltpu.VMEM((8 * NODES, elements), F32),
            pltpu.VMEM((2, 8, NODES, elements), jnp.bfloat16),
            pltpu.VMEM((8, NODES + 8, elements), F32),
            pltpu.VMEM((8, 8, 8), F32),
            pltpu.VMEM((3, elements), F32),
            pltpu.VMEM((512, 256), jnp.bfloat16),
            pltpu.VMEM((2, NODES + 8, 64, 128), F32),
            pltpu.VMEM((3, NODES) + tile, F32),
            pltpu.VMEM((NODES,) + tile, F32),
            pltpu.VMEM((4,) + tile, F32),
            pltpu.VMEM((3, SEND_TILES) + tile, F32),
            pltpu.VMEM((3, RECV_TILES) + tile, F32),
            pltpu.VMEM((3, 8, 4, 128), F32),
            pltpu.VMEM((3, len(HALF_AT), 4, 128), F32),
            pltpu.SemaphoreType.DMA((3, 26)),
            pltpu.SemaphoreType.DMA((3, 26)),
            pltpu.SemaphoreType.DMA((6,)),
        ],
        compiler_params=pltpu.CompilerParams(
            collective_id=0, has_side_effects=True, vmem_limit_bytes=52 << 20
        ),
        name="adjoint_sections",
    )(*operands)
    return out.reshape(8, NODES, elements)


def solution(mesh):
    sizes = tuple(mesh.shape[axis] for axis in AXES)
    in_specs = (
        P(None, None, AXES),
        P(None, None, None, AXES),
        P(),
        P(None, AXES),
        P(),
        P("gx", "gy"),
    )
    return jax.shard_map(
        functools.partial(on_device, sizes),
        mesh=mesh,
        in_specs=in_specs,
        out_specs=P(None, None, AXES),
        check_vma=False,
    )
```

```python
import functools

import jax
import jax.numpy as jnp
import numpy as np
from jax import lax
from jax.experimental import pallas as pl
from jax.experimental.pallas import tpu as pltpu
from jax.sharding import PartitionSpec as P

EX = 2
EY = 8
EZ = 8
STEP_LENGTH = 0.05
AXES = ("gx", "gy", "gz")
STRIDES = (36, 6, 1)
MESH = pl.DeviceIdType.MESH
NODES = 216
F32 = jnp.float32


def derivative_numbers():
    points = np.array(
        [-1.0, -0.765055323929465, -0.285231516480645, 0.285231516480645, 0.765055323929465, 1.0]
    )
    legendre = (63.0 * points**5 - 70.0 * points**3 + 15.0 * points) / 8.0
    matrix = np.zeros((6, 6))
    for row_index in range(6):
        for col_index in range(6):
            if row_index != col_index:
                matrix[row_index, col_index] = (
                    legendre[row_index]
                    / legendre[col_index]
                    / (points[row_index] - points[col_index])
                )
    matrix[0, 0] = -7.5
    matrix[5, 5] = 7.5
    return matrix


DMAT = derivative_numbers()
EVEN = [[0.5 * float(DMAT[i, m] + DMAT[5 - i, m]) for m in range(3)] for i in range(3)]
ODD = [[0.5 * float(DMAT[i, m] - DMAT[5 - i, m]) for m in range(3)] for i in range(3)]

INNER = [(a, b) for a in range(1, 5) for b in range(1, 5)]
Y_GROUPS = [
    [(0, k) for k in range(6)] + INNER[0:2],
    [(5, k) for k in range(6)] + INNER[2:4],
    [(i, 0) for i in range(6)] + INNER[4:6],
    [(i, 5) for i in range(6)] + INNER[6:8],
    INNER[8:16],
]
REST = [(i, j) for i in range(1, 5) for j in range(6)]
Z_GROUPS = [
    [(0, j) for j in range(6)] + REST[0:2],
    [(5, j) for j in range(6)] + REST[2:4],
    REST[4:12],
    REST[12:20],
    REST[20:24],
]
X_HALVES = [(j, k) for j in range(5) for k in range(5)] + ["depth", "height", None]
X_TILES = 14
XL, XH, YL, YH, ZL, ZH, SEND_TILES = 0, 14, 28, 33, 38, 43, 48


def source_of(d):
    dx, dy, dz = d
    if dy == 0 and dz == 0:
        return (XL if dx < 0 else XH), X_TILES
    if dx == 0 and dz == 0:
        return (YL if dy < 0 else YH), 5
    if dx == 0 and dy == 0:
        return (ZL if dz < 0 else ZH), 5
    return (YL if dy < 0 else YH) + (2 if dz < 0 else 3), 1


def half_source_of(d):
    dx, dy, dz = d
    side = 0 if dx < 0 else 1
    if dy == 0:
        return 4 + 2 * (dz > 0) + side, (ZL if dz < 0 else ZH) + side
    return 2 * (dy > 0) + side, (YL if dy < 0 else YH) + side


def is_half(d):
    return d[0] != 0 and (d[1] != 0 or d[2] != 0)


def directions():
    every = [(x, y, z) for x in (-1, 0, 1) for y in (-1, 0, 1) for z in (-1, 0, 1) if (x, y, z) != (0, 0, 0)]

    def rank(d):
        count = sum(abs(v) for v in d)
        if count == 3:
            return 0
        if count == 2:
            return 1 if d[1] == 0 else (2 if d[2] == 0 else 3)
        return 4 if d[2] else (5 if d[1] else 6)

    return sorted(every, key=rank)


DIRECTIONS = directions()
RECV_AT = {}
RECV_TILES = 0
HALF_AT = {}
for _d in DIRECTIONS:
    if is_half(_d):
        HALF_AT[_d] = len(HALF_AT)
    else:
        RECV_AT[_d] = RECV_TILES
        RECV_TILES += source_of(_d)[1]


def pieces():
    table = {n: [] for n in range(NODES)}
    where = {h: (x // 2, 64 * (x % 2)) for x, h in enumerate(X_HALVES)}
    for f, base, p in ((1, 180, 1), (-1, 0, 0)):
        def add(j, k, half, shift, q, r):
            tile, across = where[half]
            table[base + j * 6 + k].append(((f, 0, 0), tile, across + shift, (p, q, r)))

        for j in range(5):
            for k in range(5):
                add(j, k, (j, k), 0, None, None)
        for t in range(5):
            add(5, t, (0, t), -8, "below", None)
            add(5, t, "depth", 8 * (7 - t), 7, None)
            add(t, 5, (t, 0), -1, None, "below")
            add(t, 5, "height", 7 - t, None, 7)
        add(5, 5, (0, 0), -9, "below", "below")
        add(5, 5, "depth", 8 * (7 - 5), 7, None)
        add(5, 5, "height", 7 - 8, "below", 7)
    for g, group in enumerate(Y_GROUPS):
        for s, (i, k) in enumerate(group):
            table[i * 36 + 30 + k].append(((0, 1, 0), g, 8 * (7 - s), (None, 7, None)))
            table[i * 36 + k].append(((0, -1, 0), g, -8 * s, (None, 0, None)))
    for g, group in enumerate(Z_GROUPS):
        for s, (i, j) in enumerate(group):
            table[i * 36 + j * 6 + 5].append(((0, 0, 1), g, 7 - s, (None, None, 7)))
            table[i * 36 + j * 6].append(((0, 0, -1), g, -s, (None, None, 0)))
    return table


HALF_FROM = dict(half_source_of(d) for d in DIRECTIONS if is_half(d))
PIECES = pieces()
BOUNDARY = [n for n in range(NODES) if PIECES[n]]
INTERIOR = [n for n in range(NODES) if not PIECES[n]]


def roll(x, shift):
    shift = shift % 128
    return x if shift == 0 else pltpu.roll(x, shift, 1)


def exists(d, sizes):
    ok = None
    for axis, off, size in zip(AXES, d, sizes):
        if off == 0:
            continue
        here = lax.axis_index(axis)
        term = here < size - 1 if off > 0 else here > 0
        ok = term if ok is None else jnp.logical_and(ok, term)
    return ok


def device_at(d):
    return {axis: lax.axis_index(axis) + off for axis, off in zip(AXES, d) if off != 0}


def kernel(
    sizes, cost_hbm, state_hbm, rates_hbm, motion_hbm, drift_hbm, flags_hbm, out_ref,
    drift_ref, flags_ref, stage, state_v, state_f, rates_v, motion_v, mix_lhs, mix, X, T, consts,
    send_buf, recv_buf, send_half, recv_half, send_sem, recv_sem, load_sem,
):
    lane = lax.broadcasted_iota(jnp.int32, (8, 128), 1)
    sub = lax.broadcasted_iota(jnp.int32, (8, 128), 0)
    p_at, q_at, r_at = lane // 64, (lane // 8) % 8, lane % 8

    loads = [
        pltpu.make_async_copy(cost_hbm, stage, load_sem.at[0]),
        pltpu.make_async_copy(motion_hbm, motion_v, load_sem.at[1]),
        pltpu.make_async_copy(rates_hbm, rates_v, load_sem.at[2]),
        pltpu.make_async_copy(state_hbm, state_v, load_sem.at[3]),
        pltpu.make_async_copy(drift_hbm, drift_ref, load_sem.at[4]),
        pltpu.make_async_copy(flags_hbm, flags_ref, load_sem.at[5]),
    ]
    for load in loads:
        load.start()

    barrier = pltpu.get_barrier_semaphore()
    for d in DIRECTIONS:
        @pl.when(exists(d, sizes))
        def _():
            pl.semaphore_signal(barrier, inc=1, device_id=device_at(d), device_id_type=MESH)

    for d in DIRECTIONS:
        @pl.when(jnp.logical_not(exists(tuple(-v for v in d), sizes)))
        def _():
            for s in range(3):
                if is_half(d):
                    recv_half[s, HALF_AT[d]] = jnp.zeros((4, 128), F32)
                else:
                    n = source_of(d)[1]
                    recv_buf[s, pl.ds(RECV_AT[d], n)] = jnp.zeros((n, 8, 128), F32)

    loads[5].wait()
    keep = jnp.ones((8, 128), F32)
    bottom = lax.axis_index("gz") == 0
    for p in range(EX):
        for q in range(EY):
            open_here = 1.0 - flags_ref[p, q].astype(F32)
            hit = jnp.logical_and(lane == p * 64 + q * 8, bottom)
            keep = jnp.where(hit, open_here, keep)
    consts[0] = keep

    def sweep(ref, d):
        a_d, b_d = [x for x in range(3) if x != d]
        shift = (64, 8, 1)[d]
        at = (p_at, q_at, r_at)[d]
        last = (1, 7, 7)[d]

        for t in range(6):
            for u in range(6):
                lo_n = t * STRIDES[a_d] + u * STRIDES[b_d]
                hi_n = lo_n + 5 * STRIDES[d]
                a, b = ref[lo_n], ref[hi_n]
                if d == 0:
                    both = jnp.where(at == 1, a, b)
                    both = both + roll(both, 64)
                    ref[lo_n] = jnp.where(at == 1, both, a)
                    ref[hi_n] = jnp.where(at == 0, both, b)
                else:
                    s = a + roll(b, shift)
                    ref[lo_n] = jnp.where(at > 0, s, a)
                    ref[hi_n] = jnp.where(at < last, roll(s, -shift), b)

    def pack_faces(slot):
        for g, group in enumerate(Y_GROUPS):
            low = high = jnp.zeros((8, 128), F32)
            for s, (i, k) in enumerate(group):
                low = jnp.where(q_at == s, roll(T[i * 36 + k], 8 * s), low)
                high = jnp.where(q_at == s, roll(T[i * 36 + 30 + k], 8 * (s - 7)), high)
            send_buf[slot, YL + g] = low
            send_buf[slot, YH + g] = high
        for g, group in enumerate(Z_GROUPS):
            low = high = jnp.zeros((8, 128), F32)
            for s, (i, j) in enumerate(group):
                low = jnp.where(r_at == s, roll(T[i * 36 + j * 6], s), low)
                high = jnp.where(r_at == s, roll(T[i * 36 + j * 6 + 5], s - 7), high)
            send_buf[slot, ZL + g] = low
            send_buf[slot, ZH + g] = high

        for at in range(8):
            full = send_buf[slot, HALF_FROM[at]]
            other = roll(pltpu.roll(full, 4, 0), 64)
            send_half[slot, at] = jnp.where(p_at == at % 2, full, other)[0:4]

    def pack_width(slot):
        def half(h, high):
            if h == "depth":
                return send_buf[slot, YH + high]
            if h == "height":
                return send_buf[slot, ZH + high]
            return T[180 * high + h[0] * 6 + h[1]]

        for t in range(X_TILES):
            for high, at in ((0, XL), (1, XH)):
                tile = roll(half(X_HALVES[2 * t], high), 64)
                if X_HALVES[2 * t + 1] is not None:
                    tile = jnp.where(p_at == 1 - high, tile, half(X_HALVES[2 * t + 1], high))
                send_buf[slot, at + t] = tile

    def message(slot, m):
        d = DIRECTIONS[m]
        if is_half(d):
            src = send_half.at[slot, half_source_of(d)[0]]
            dst = recv_half.at[slot, HALF_AT[d]]
        else:
            at, n = source_of(d)
            src = send_buf.at[slot, pl.ds(at, n)]
            dst = recv_buf.at[slot, pl.ds(RECV_AT[d], n)]
        return pltpu.make_async_remote_copy(
            src_ref=src,
            dst_ref=dst,
            send_sem=send_sem.at[slot, m],
            recv_sem=recv_sem.at[slot, m],
            device_id=device_at(d),
            device_id_type=MESH,
        )

    def start(slot, width):
        for m, d in enumerate(DIRECTIONS):
            if (d[1] == 0 and d[2] == 0) == width:
                @pl.when(exists(d, sizes))
                def _():
                    message(slot, m).start()

    def send(slot):
        pack_faces(slot)
        start(slot, False)
        pack_width(slot)
        start(slot, True)

    def wait_sent(slot):
        for m, d in enumerate(DIRECTIONS):
            @pl.when(exists(d, sizes))
            def _():
                message(slot, m).wait_send()

    def wait_received(slot, across):
        for m, d in enumerate(DIRECTIONS):
            if (d[0] != 0) == across:
                @pl.when(exists(tuple(-v for v in d), sizes))
                def _():
                    message(slot, m).wait_recv()

    def got(slot, f, tile=0):
        return recv_buf[slot, RECV_AT[tuple(-v for v in f)] + tile]

    def got_half(slot, f):
        part = recv_half[slot, HALF_AT[tuple(-v for v in f)]]
        return jnp.concatenate([roll(part, 64), part], axis=0)

    def join(slot, across):
        zero = jnp.zeros((8, 128), F32)
        for fy in (1, -1):
            for g in (0, 1) if across else (2, 3):
                v = got(slot, (0, fy, 0), g)
                if g < 2:
                    fx = 1 if g == 1 else -1
                    mine = jnp.logical_and(p_at == (1 if fx > 0 else 0), q_at < 6)
                    v = v + jnp.where(mine, got_half(slot, (fx, fy, 0)), zero)
                    for fz in (1, -1):
                        target = (64 if fx > 0 else 0) + (47 if fz > 0 else 0)
                        origin = (0 if fx > 0 else 64) + (0 if fz > 0 else 47)
                        corner = roll(got_half(slot, (fx, fy, fz)), target - origin - 64)
                        v = v + jnp.where(lane == target, corner, zero)
                else:
                    fz = 1 if g == 3 else -1
                    v = jnp.where(jnp.logical_or(q_at == 0, q_at == 5), zero, v)
                    mine = jnp.logical_and(r_at == (7 if fz > 0 else 0), q_at < 6)
                    v = v + jnp.where(mine, roll(got(slot, (0, fy, fz)), 7 * fz), zero)
                recv_buf[slot, RECV_AT[(0, -fy, 0)] + g] = v
        for fz in (1, -1) if across else ():
            for g in range(2):
                fx = 1 if g == 1 else -1
                mine = jnp.logical_and(p_at == (1 if fx > 0 else 0), r_at < 6)
                v = got(slot, (0, 0, fz), g) + jnp.where(mine, got_half(slot, (fx, 0, fz)), zero)
                recv_buf[slot, RECV_AT[(0, 0, -fz)] + g] = v

    def masked(places):
        mask = None
        for at, place in zip((p_at, q_at, r_at), places):
            if place is not None:
                term = at < 7 if place == "below" else at == place
                mask = term if mask is None else jnp.logical_and(mask, term)
        return mask

    def unpack(slot, across, put):
        wait_received(slot, across)
        join(slot, across)
        zero = jnp.zeros((8, 128), F32)
        for n in BOUNDARY:
            if (n // 36 in (0, 5)) != across:
                continue
            value = X[slot, n]
            for f, tile, shift, places in PIECES[n]:
                value = value + jnp.where(masked(places), roll(got(slot, f, tile), shift), zero)
            put(n, value)

    def line(r, base, d, outputs, masks_bottom=False):
        stride = STRIDES[d]
        h = [X[r, base + m * stride] for m in range(6)]
        even = [h[i] + h[5 - i] for i in range(3)]
        odd = [h[i] - h[5 - i] for i in range(3)]
        speed = consts[1 + d]
        for m in outputs:
            pe = EVEN[0][m] * even[0] + EVEN[1][m] * even[1] + EVEN[2][m] * even[2]
            qo = ODD[0][m] * odd[0] + ODD[1][m] * odd[1] + ODD[2][m] * odd[2]
            for at, value in ((m, qo + pe), (5 - m, qo - pe)):
                n = base + at * stride
                value = speed * value
                if d != 1:
                    value = value + T[n]
                if d == 2:
                    for a in range(8):
                        value = value + mix[1 - r, n, pl.ds(8 * a, 8), :] * X[r, n, pl.ds(a, 1), :]
                if masks_bottom:
                    value = value * consts[0]
                T[n] = value

    def planes(r, which):
        for d in (1, 2):
            for i in which:
                for t in range(6):
                    line(r, i * 36 + t * STRIDES[3 - d], d, (0, 1, 2))

    def width_lines(r, boundary):
        for j in range(6):
            for k in range(6):
                whole = j in (0, 5) or k in (0, 5)
                if boundary:
                    line(r, j * 6 + k, 0, (0, 1, 2) if whole else (0,), k == 0)
                elif not whole:
                    line(r, j * 6 + k, 0, (1, 2))

    def settle():
        for d in range(3):
            sweep(T, d)

    loads[1].wait()
    loads[4].wait()
    drift = jnp.zeros((8, 128), F32)
    for c in range(8):
        drift = jnp.where(sub == c, drift_ref[c], drift)
    for d in range(3):
        pace = jnp.broadcast_to(motion_v[pl.ds(d, 1), :], (8, 128))
        if d == 2:
            pace = pace + drift
        consts[1 + d] = -STEP_LENGTH * pace

    loads[0].wait()

    def fetch(t, _):
        for k in range(36):
            n = t * 36 + k
            v = stage[pl.ds(n, 8, stride=NODES), :]
            T[n] = v * keep if k % 6 == 0 else v
        return 0

    lax.fori_loop(0, 6, fetch, 0)
    settle()
    count = 1
    for axis, size in zip(AXES, sizes):
        here = lax.axis_index(axis)
        count = count * (1 + (here > 0).astype(jnp.int32) + (here < size - 1).astype(jnp.int32))
    pl.semaphore_wait(barrier, count - 1)
    send(0)

    def copy_over(t, _):
        for v in range(24):
            X[0, t * 24 + v] = T[t * 24 + v]
        return 0

    lax.fori_loop(0, 9, copy_over, 0)
    loads[2].wait()
    loads[3].wait()
    highest = lax.Precision.HIGHEST
    spread = (
        lax.broadcasted_iota(jnp.int32, (8, 256), 1) // 8 % 8
        == lax.broadcasted_iota(jnp.int32, (8, 256), 0)
    ).astype(F32)
    rows = []
    for a in range(8):
        block = rates_v[a]
        straight = jnp.dot(block, spread, precision=highest, preferred_element_type=F32)
        turned = lax.dot_general(
            block, spread, (((0,), (0,)), ((), ())), precision=highest, preferred_element_type=F32
        )
        rows.append(straight + turned)
    weights = STEP_LENGTH * jnp.concatenate(rows, axis=0)
    column = lax.broadcasted_iota(jnp.int32, (64, 256), 1)
    first = weights.astype(jnp.bfloat16).astype(F32)
    second = (weights - first).astype(jnp.bfloat16).astype(F32)
    third = (weights - first) - second
    parts = jnp.where(
        column < 64, first, jnp.where(column < 128, second, jnp.where(column < 192, third, 0.0))
    )
    for m in range(8):
        mix_lhs[pl.ds(64 * m, 64), :] = jnp.where(column % 8 == m, parts, 0.0).astype(jnp.bfloat16)

    def contract(s):
        for b in range(8):
            state_f[b, pl.ds(0, NODES)] = state_v[s, b].astype(F32)

        def body(g, _):
            base = pl.multiple_of(16 * g, 16)
            halves = []
            for half in range(2):
                block = state_f[:, pl.ds(base + 8 * half, 8), :]
                halves.append(block.reshape(64, 128).astype(jnp.bfloat16))
            both = jnp.concatenate(halves, axis=1)
            stacked = jnp.concatenate([both] * 4, axis=0)
            res = jnp.dot(mix_lhs[...], stacked, preferred_element_type=F32)
            for half in range(2):
                mix[s, pl.ds(base + 8 * half, 8)] = res[:, 128 * half : 128 * half + 128].reshape(8, 64, 128)
            return 0

        lax.fori_loop(0, 14, body, 0)

    state_f[:, pl.ds(NODES, 8), :] = jnp.zeros((8, 8, 128), F32)
    contract(1)
    wait_sent(0)

    def section(r, _):
        def keep_value(n, value):
            X[r, n] = value

        unpack(r, False, keep_value)
        planes(r, (1, 2, 3, 4))
        unpack(r, True, keep_value)
        planes(r, (0, 5))
        width_lines(r, True)
        settle()
        send(r + 1)
        width_lines(r, False)
        weight = r.astype(F32)

        def gather(t, _):
            for v in range(24):
                n = t * 24 + v
                X[r + 1, n] = X[0, n] + weight * X[r, n] + T[n]
            return 0

        lax.fori_loop(0, 9, gather, 0)

        @pl.when(r == 0)
        def _():
            contract(0)

        wait_sent(r + 1)
        return 0

    lax.fori_loop(0, 2, section, 0)

    def emit(n, value):
        out_ref[pl.ds(n, 8, stride=NODES), :] = 0.5 * value

    for n in INTERIOR:
        emit(n, X[2, n])
    unpack(2, False, emit)
    unpack(2, True, emit)


def on_device(sizes, cost, states, rates, motion, drift, flags):
    elements = EX * EY * EZ
    hbm = pl.BlockSpec(memory_space=pltpu.HBM)
    operands = [
        pltpu.with_memory_space_constraint(x, pltpu.HBM)
        for x in (cost.reshape(8 * NODES, elements), states, rates, motion, drift, flags)
    ]
    tile = (8, 128)
    out = pl.pallas_call(
        functools.partial(kernel, sizes),
        out_shape=pltpu.VMEM((8 * NODES, elements), F32),
        in_specs=[hbm] * 6,
        out_specs=pl.BlockSpec(memory_space=pltpu.VMEM),
        scratch_shapes=[
            pltpu.SMEM((8,), F32),
            pltpu.SMEM((EX, EY), jnp.int32),
            pltpu.VMEM((8 * NODES, elements), F32),
            pltpu.VMEM((2, 8, NODES, elements), jnp.bfloat16),
            pltpu.VMEM((8, NODES + 8, elements), F32),
            pltpu.VMEM((8, 8, 8), F32),
            pltpu.VMEM((3, elements), F32),
            pltpu.VMEM((512, 256), jnp.bfloat16),
            pltpu.VMEM((2, NODES + 8, 64, 128), F32),
            pltpu.VMEM((3, NODES) + tile, F32),
            pltpu.VMEM((NODES,) + tile, F32),
            pltpu.VMEM((4,) + tile, F32),
            pltpu.VMEM((3, SEND_TILES) + tile, F32),
            pltpu.VMEM((3, RECV_TILES) + tile, F32),
            pltpu.VMEM((3, 8, 4, 128), F32),
            pltpu.VMEM((3, len(HALF_AT), 4, 128), F32),
            pltpu.SemaphoreType.DMA((3, 26)),
            pltpu.SemaphoreType.DMA((3, 26)),
            pltpu.SemaphoreType.DMA((6,)),
        ],
        compiler_params=pltpu.CompilerParams(
            collective_id=0, has_side_effects=True, vmem_limit_bytes=52 << 20
        ),
        name="adjoint_sections",
    )(*operands)
    return out.reshape(8, NODES, elements)


def solution(mesh):
    sizes = tuple(mesh.shape[axis] for axis in AXES)
    in_specs = (
        P(None, None, AXES),
        P(None, None, None, AXES),
        P(),
        P(None, AXES),
        P(),
        P("gx", "gy"),
    )
    return jax.shard_map(
        functools.partial(on_device, sizes),
        mesh=mesh,
        in_specs=in_specs,
        out_specs=P(None, None, AXES),
        check_vma=False,
    )
```

```python
import functools

import jax
import jax.numpy as jnp
import numpy as np
from jax import lax
from jax.experimental import pallas as pl
from jax.experimental.pallas import tpu as pltpu
from jax.sharding import PartitionSpec as P

EX = 2
EY = 8
EZ = 8
STEP_LENGTH = 0.05
AXES = ("gx", "gy", "gz")
STRIDES = (36, 6, 1)
MESH = pl.DeviceIdType.MESH
NODES = 216
F32 = jnp.float32


def derivative_numbers():
    points = np.array(
        [-1.0, -0.765055323929465, -0.285231516480645, 0.285231516480645, 0.765055323929465, 1.0]
    )
    legendre = (63.0 * points**5 - 70.0 * points**3 + 15.0 * points) / 8.0
    matrix = np.zeros((6, 6))
    for row_index in range(6):
        for col_index in range(6):
            if row_index != col_index:
                matrix[row_index, col_index] = (
                    legendre[row_index]
                    / legendre[col_index]
                    / (points[row_index] - points[col_index])
                )
    matrix[0, 0] = -7.5
    matrix[5, 5] = 7.5
    return matrix


DMAT = derivative_numbers()
EVEN = [[0.5 * float(DMAT[i, m] + DMAT[5 - i, m]) for m in range(3)] for i in range(3)]
ODD = [[0.5 * float(DMAT[i, m] - DMAT[5 - i, m]) for m in range(3)] for i in range(3)]

INNER = [(a, b) for a in range(1, 5) for b in range(1, 5)]
Y_GROUPS = [
    [(0, k) for k in range(6)] + INNER[0:2],
    [(5, k) for k in range(6)] + INNER[2:4],
    [(i, 0) for i in range(6)] + INNER[4:6],
    [(i, 5) for i in range(6)] + INNER[6:8],
    INNER[8:16],
]
REST = [(i, j) for i in range(1, 5) for j in range(6)]
Z_GROUPS = [
    [(0, j) for j in range(6)] + REST[0:2],
    [(5, j) for j in range(6)] + REST[2:4],
    REST[4:12],
    REST[12:20],
    REST[20:24],
]
X_HALVES = [(j, k) for j in range(5) for k in range(5)] + ["depth", "height", None]
X_TILES = 14
XL, XH, YL, YH, ZL, ZH, SEND_TILES = 0, 14, 28, 33, 38, 43, 48


def source_of(d):
    dx, dy, dz = d
    if dy == 0 and dz == 0:
        return (XL if dx < 0 else XH), X_TILES
    if dx == 0 and dz == 0:
        return (YL if dy < 0 else YH), 5
    if dx == 0 and dy == 0:
        return (ZL if dz < 0 else ZH), 5
    return (YL if dy < 0 else YH) + (2 if dz < 0 else 3), 1


def half_source_of(d):
    dx, dy, dz = d
    side = 0 if dx < 0 else 1
    if dy == 0:
        return 4 + 2 * (dz > 0) + side, (ZL if dz < 0 else ZH) + side
    return 2 * (dy > 0) + side, (YL if dy < 0 else YH) + side


def is_half(d):
    return d[0] != 0 and (d[1] != 0 or d[2] != 0)


def directions():
    every = [(x, y, z) for x in (-1, 0, 1) for y in (-1, 0, 1) for z in (-1, 0, 1) if (x, y, z) != (0, 0, 0)]

    def rank(d):
        count = sum(abs(v) for v in d)
        if count == 3:
            return 0
        if count == 2:
            return 1 if d[1] == 0 else (2 if d[2] == 0 else 3)
        return 4 if d[2] else (5 if d[1] else 6)

    return sorted(every, key=rank)


DIRECTIONS = directions()
RECV_AT = {}
RECV_TILES = 0
HALF_AT = {}
for _d in DIRECTIONS:
    if is_half(_d):
        HALF_AT[_d] = len(HALF_AT)
    else:
        RECV_AT[_d] = RECV_TILES
        RECV_TILES += source_of(_d)[1]


def pieces():
    table = {n: [] for n in range(NODES)}
    where = {h: (x // 2, 64 * (x % 2)) for x, h in enumerate(X_HALVES)}
    for f, base, p in ((1, 180, 1), (-1, 0, 0)):
        def add(j, k, half, shift, q, r):
            tile, across = where[half]
            table[base + j * 6 + k].append(((f, 0, 0), tile, across + shift, (p, q, r)))

        for j in range(5):
            for k in range(5):
                add(j, k, (j, k), 0, None, None)
        for t in range(5):
            add(5, t, (0, t), -8, "below", None)
            add(5, t, "depth", 8 * (7 - t), 7, None)
            add(t, 5, (t, 0), -1, None, "below")
            add(t, 5, "height", 7 - t, None, 7)
        add(5, 5, (0, 0), -9, "below", "below")
        add(5, 5, "depth", 8 * (7 - 5), 7, None)
        add(5, 5, "height", 7 - 8, "below", 7)
    for g, group in enumerate(Y_GROUPS):
        for s, (i, k) in enumerate(group):
            table[i * 36 + 30 + k].append(((0, 1, 0), g, 8 * (7 - s), (None, 7, None)))
            table[i * 36 + k].append(((0, -1, 0), g, -8 * s, (None, 0, None)))
    for g, group in enumerate(Z_GROUPS):
        for s, (i, j) in enumerate(group):
            table[i * 36 + j * 6 + 5].append(((0, 0, 1), g, 7 - s, (None, None, 7)))
            table[i * 36 + j * 6].append(((0, 0, -1), g, -s, (None, None, 0)))
    return table


HALF_FROM = dict(half_source_of(d) for d in DIRECTIONS if is_half(d))
PIECES = pieces()
BOUNDARY = [n for n in range(NODES) if PIECES[n]]
INTERIOR = [n for n in range(NODES) if not PIECES[n]]


def roll(x, shift):
    shift = shift % 128
    return x if shift == 0 else pltpu.roll(x, shift, 1)


def exists(d, sizes):
    ok = None
    for axis, off, size in zip(AXES, d, sizes):
        if off == 0:
            continue
        here = lax.axis_index(axis)
        term = here < size - 1 if off > 0 else here > 0
        ok = term if ok is None else jnp.logical_and(ok, term)
    return ok


def device_at(d):
    return {axis: lax.axis_index(axis) + off for axis, off in zip(AXES, d) if off != 0}


def kernel(
    sizes, cost_hbm, state_hbm, rates_hbm, motion_hbm, drift_hbm, flags_hbm, out_ref,
    drift_ref, flags_ref, stage, state_v, state_f, rates_v, motion_v, mix_lhs, mix, X, T, consts,
    send_buf, recv_buf, send_half, recv_half, send_sem, recv_sem, load_sem,
):
    lane = lax.broadcasted_iota(jnp.int32, (8, 128), 1)
    sub = lax.broadcasted_iota(jnp.int32, (8, 128), 0)
    p_at, q_at, r_at = lane // 64, (lane // 8) % 8, lane % 8

    barrier = pltpu.get_barrier_semaphore()
    for d in DIRECTIONS:
        @pl.when(exists(d, sizes))
        def _():
            pl.semaphore_signal(barrier, inc=1, device_id=device_at(d), device_id_type=MESH)

    loads = [
        pltpu.make_async_copy(cost_hbm, stage, load_sem.at[0]),
        pltpu.make_async_copy(motion_hbm, motion_v, load_sem.at[1]),
        pltpu.make_async_copy(rates_hbm, rates_v, load_sem.at[2]),
        pltpu.make_async_copy(state_hbm, state_v, load_sem.at[3]),
        pltpu.make_async_copy(drift_hbm, drift_ref, load_sem.at[4]),
        pltpu.make_async_copy(flags_hbm, flags_ref, load_sem.at[5]),
    ]
    for load in loads:
        load.start()

    for d in DIRECTIONS:
        @pl.when(jnp.logical_not(exists(tuple(-v for v in d), sizes)))
        def _():
            for s in range(3):
                if is_half(d):
                    recv_half[s, HALF_AT[d]] = jnp.zeros((4, 128), F32)
                else:
                    n = source_of(d)[1]
                    recv_buf[s, pl.ds(RECV_AT[d], n)] = jnp.zeros((n, 8, 128), F32)

    loads[5].wait()
    keep = jnp.ones((8, 128), F32)
    bottom = lax.axis_index("gz") == 0
    for p in range(EX):
        for q in range(EY):
            open_here = 1.0 - flags_ref[p, q].astype(F32)
            hit = jnp.logical_and(lane == p * 64 + q * 8, bottom)
            keep = jnp.where(hit, open_here, keep)
    consts[0] = keep

    def sweep(ref, d, needed):
        a_d, b_d = [x for x in range(3) if x != d]
        shift = (64, 8, 1)[d]
        at = (p_at, q_at, r_at)[d]
        last = (1, 7, 7)[d]

        for t in range(6):
            for u in range(6):
                if (t in (0, 5) or u in (0, 5)) != needed:
                    continue
                lo_n = t * STRIDES[a_d] + u * STRIDES[b_d]
                hi_n = lo_n + 5 * STRIDES[d]
                a, b = ref[lo_n], ref[hi_n]
                if d == 0:
                    both = jnp.where(at == 1, a, b)
                    both = both + roll(both, 64)
                    ref[lo_n] = jnp.where(at == 1, both, a)
                    ref[hi_n] = jnp.where(at == 0, both, b)
                else:
                    s = a + roll(b, shift)
                    ref[lo_n] = jnp.where(at > 0, s, a)
                    ref[hi_n] = jnp.where(at < last, roll(s, -shift), b)

    def pack_faces(slot):
        for g, group in enumerate(Y_GROUPS):
            low = high = jnp.zeros((8, 128), F32)
            for s, (i, k) in enumerate(group):
                low = jnp.where(q_at == s, roll(T[i * 36 + k], 8 * s), low)
                high = jnp.where(q_at == s, roll(T[i * 36 + 30 + k], 8 * (s - 7)), high)
            send_buf[slot, YL + g] = low
            send_buf[slot, YH + g] = high
        for g, group in enumerate(Z_GROUPS):
            low = high = jnp.zeros((8, 128), F32)
            for s, (i, j) in enumerate(group):
                low = jnp.where(r_at == s, roll(T[i * 36 + j * 6], s), low)
                high = jnp.where(r_at == s, roll(T[i * 36 + j * 6 + 5], s - 7), high)
            send_buf[slot, ZL + g] = low
            send_buf[slot, ZH + g] = high

        for at in range(8):
            full = send_buf[slot, HALF_FROM[at]]
            other = roll(pltpu.roll(full, 4, 0), 64)
            send_half[slot, at] = jnp.where(p_at == at % 2, full, other)[0:4]

    def pack_width(slot):
        def half(h, high):
            if h == "depth":
                return send_buf[slot, YH + high]
            if h == "height":
                return send_buf[slot, ZH + high]
            return T[180 * high + h[0] * 6 + h[1]]

        for t in range(X_TILES):
            for high, at in ((0, XL), (1, XH)):
                tile = roll(half(X_HALVES[2 * t], high), 64)
                if X_HALVES[2 * t + 1] is not None:
                    tile = jnp.where(p_at == 1 - high, tile, half(X_HALVES[2 * t + 1], high))
                send_buf[slot, at + t] = tile

    def message(slot, m):
        d = DIRECTIONS[m]
        if is_half(d):
            src = send_half.at[slot, half_source_of(d)[0]]
            dst = recv_half.at[slot, HALF_AT[d]]
        else:
            at, n = source_of(d)
            src = send_buf.at[slot, pl.ds(at, n)]
            dst = recv_buf.at[slot, pl.ds(RECV_AT[d], n)]
        return pltpu.make_async_remote_copy(
            src_ref=src,
            dst_ref=dst,
            send_sem=send_sem.at[slot, m],
            recv_sem=recv_sem.at[slot, m],
            device_id=device_at(d),
            device_id_type=MESH,
        )

    def start(slot, width):
        for m, d in enumerate(DIRECTIONS):
            if (d[1] == 0 and d[2] == 0) == width:
                @pl.when(exists(d, sizes))
                def _():
                    message(slot, m).start()

    def send(slot):
        pack_faces(slot)
        start(slot, False)
        pack_width(slot)
        start(slot, True)

    def wait_sent(slot):
        for m, d in enumerate(DIRECTIONS):
            @pl.when(exists(d, sizes))
            def _():
                message(slot, m).wait_send()

    def wait_received(slot, across):
        for m, d in enumerate(DIRECTIONS):
            if (d[0] != 0) == across:
                @pl.when(exists(tuple(-v for v in d), sizes))
                def _():
                    message(slot, m).wait_recv()

    def got(slot, f, tile=0):
        return recv_buf[slot, RECV_AT[tuple(-v for v in f)] + tile]

    def got_half(slot, f):
        part = recv_half[slot, HALF_AT[tuple(-v for v in f)]]
        return jnp.concatenate([roll(part, 64), part], axis=0)

    def join(slot, across):
        zero = jnp.zeros((8, 128), F32)
        for fy in (1, -1):
            for g in (0, 1) if across else (2, 3):
                v = got(slot, (0, fy, 0), g)
                if g < 2:
                    fx = 1 if g == 1 else -1
                    mine = jnp.logical_and(p_at == (1 if fx > 0 else 0), q_at < 6)
                    v = v + jnp.where(mine, got_half(slot, (fx, fy, 0)), zero)
                    for fz in (1, -1):
                        target = (64 if fx > 0 else 0) + (47 if fz > 0 else 0)
                        origin = (0 if fx > 0 else 64) + (0 if fz > 0 else 47)
                        corner = roll(got_half(slot, (fx, fy, fz)), target - origin - 64)
                        v = v + jnp.where(lane == target, corner, zero)
                else:
                    fz = 1 if g == 3 else -1
                    v = jnp.where(jnp.logical_or(q_at == 0, q_at == 5), zero, v)
                    mine = jnp.logical_and(r_at == (7 if fz > 0 else 0), q_at < 6)
                    v = v + jnp.where(mine, roll(got(slot, (0, fy, fz)), 7 * fz), zero)
                recv_buf[slot, RECV_AT[(0, -fy, 0)] + g] = v
        for fz in (1, -1) if across else ():
            for g in range(2):
                fx = 1 if g == 1 else -1
                mine = jnp.logical_and(p_at == (1 if fx > 0 else 0), r_at < 6)
                v = got(slot, (0, 0, fz), g) + jnp.where(mine, got_half(slot, (fx, 0, fz)), zero)
                recv_buf[slot, RECV_AT[(0, 0, -fz)] + g] = v

    def masked(places):
        mask = None
        for at, place in zip((p_at, q_at, r_at), places):
            if place is not None:
                term = at < 7 if place == "below" else at == place
                mask = term if mask is None else jnp.logical_and(mask, term)
        return mask

    def unpack(slot, across, put):
        wait_received(slot, across)
        join(slot, across)
        zero = jnp.zeros((8, 128), F32)
        for n in BOUNDARY:
            if (n // 36 in (0, 5)) != across:
                continue
            value = X[slot, n]
            for f, tile, shift, places in PIECES[n]:
                value = value + jnp.where(masked(places), roll(got(slot, f, tile), shift), zero)
            put(n, value)

    def line(r, base, d, add):
        stride = STRIDES[d]
        h = [X[r, base + m * stride] for m in range(6)]
        even = [h[i] + h[5 - i] for i in range(3)]
        odd = [h[i] - h[5 - i] for i in range(3)]
        speed = consts[1 + d]
        for m in range(3):
            pe = EVEN[0][m] * even[0] + EVEN[1][m] * even[1] + EVEN[2][m] * even[2]
            qo = ODD[0][m] * odd[0] + ODD[1][m] * odd[1] + ODD[2][m] * odd[2]
            for at, value in ((m, qo + pe), (5 - m, qo - pe)):
                n = base + at * stride
                value = speed * value
                if add:
                    value = value + T[n]
                if d == 2:
                    for a in range(8):
                        value = value + mix[1 - r, n, pl.ds(8 * a, 8), :] * X[r, n, pl.ds(a, 1), :]
                T[n] = value

    def planes(r, which):
        for d in (1, 2):
            for i in which:
                for t in range(6):
                    line(r, i * 36 + t * STRIDES[3 - d], d, d == 2 or i in (0, 5))

    def width_inside(r):
        speed = consts[1]
        for n in range(36):
            h = [X[r, n + 36 * i] for i in range(1, 5)]
            even, odd = (h[0] + h[3], h[1] + h[2]), (h[0] - h[3], h[1] - h[2])
            for m in range(3):
                pe = EVEN[1][m] * even[0] + EVEN[2][m] * even[1]
                qo = ODD[1][m] * odd[0] + ODD[2][m] * odd[1]
                for at, value in ((m, qo + pe), (5 - m, qo - pe)):
                    value = speed * value
                    T[n + 36 * at] = value if m == 0 else value + T[n + 36 * at]

    def width_ends(r, boundary):
        speed = consts[1]
        for j in range(6):
            for k in range(6):
                n = j * 6 + k
                whole = j in (0, 5) or k in (0, 5)
                if whole and not boundary:
                    continue
                first, last = X[r, n], X[r, n + 180]
                even, odd = speed * (first + last), speed * (first - last)
                for m in range(3):
                    if not whole and (m == 0) != boundary:
                        continue
                    pe, qo = EVEN[0][m] * even, ODD[0][m] * odd
                    for at, value in ((m, qo + pe), (5 - m, qo - pe)):
                        value = value + T[n + 36 * at]
                        T[n + 36 * at] = value * consts[0] if k == 0 else value

    def settle(needed):
        for d in range(3):
            sweep(T, d, needed)

    loads[1].wait()
    loads[4].wait()
    drift = jnp.zeros((8, 128), F32)
    for c in range(8):
        drift = jnp.where(sub == c, drift_ref[c], drift)
    for d in range(3):
        pace = jnp.broadcast_to(motion_v[pl.ds(d, 1), :], (8, 128))
        if d == 2:
            pace = pace + drift
        consts[1 + d] = -STEP_LENGTH * pace

    loads[0].wait()

    def fetch(t, _):
        for k in range(36):
            n = t * 36 + k
            v = stage[pl.ds(n, 8, stride=NODES), :]
            T[n] = v * keep if k % 6 == 0 else v
        return 0

    lax.fori_loop(0, 6, fetch, 0)
    settle(True)
    pack_faces(0)
    pack_width(0)
    count = 1
    for axis, size in zip(AXES, sizes):
        here = lax.axis_index(axis)
        count = count * (1 + (here > 0).astype(jnp.int32) + (here < size - 1).astype(jnp.int32))
    pl.semaphore_wait(barrier, count - 1)
    start(0, False)
    start(0, True)
    settle(False)

    def copy_over(t, _):
        for v in range(24):
            X[0, t * 24 + v] = T[t * 24 + v]
        return 0

    lax.fori_loop(0, 9, copy_over, 0)
    loads[2].wait()
    loads[3].wait()
    highest = lax.Precision.HIGHEST
    spread = (
        lax.broadcasted_iota(jnp.int32, (8, 256), 1) // 8 % 8
        == lax.broadcasted_iota(jnp.int32, (8, 256), 0)
    ).astype(F32)
    rows = []
    for a in range(8):
        block = rates_v[a]
        straight = jnp.dot(block, spread, precision=highest, preferred_element_type=F32)
        turned = lax.dot_general(
            block, spread, (((0,), (0,)), ((), ())), precision=highest, preferred_element_type=F32
        )
        rows.append(straight + turned)
    weights = STEP_LENGTH * jnp.concatenate(rows, axis=0)
    column = lax.broadcasted_iota(jnp.int32, (64, 256), 1)
    first = weights.astype(jnp.bfloat16).astype(F32)
    second = (weights - first).astype(jnp.bfloat16).astype(F32)
    third = (weights - first) - second
    parts = jnp.where(
        column < 64, first, jnp.where(column < 128, second, jnp.where(column < 192, third, 0.0))
    )
    for m in range(8):
        mix_lhs[pl.ds(64 * m, 64), :] = jnp.where(column % 8 == m, parts, 0.0).astype(jnp.bfloat16)

    def contract(s):
        for b in range(8):
            state_f[b, pl.ds(0, NODES)] = state_v[s, b].astype(F32)

        def body(g, _):
            base = pl.multiple_of(16 * g, 16)
            halves = []
            for half in range(2):
                block = state_f[:, pl.ds(base + 8 * half, 8), :]
                halves.append(block.reshape(64, 128).astype(jnp.bfloat16))
            both = jnp.concatenate(halves, axis=1)
            stacked = jnp.concatenate([both] * 4, axis=0)
            res = jnp.dot(mix_lhs[...], stacked, preferred_element_type=F32)
            for half in range(2):
                mix[s, pl.ds(base + 8 * half, 8)] = res[:, 128 * half : 128 * half + 128].reshape(8, 64, 128)
            return 0

        lax.fori_loop(0, 14, body, 0)

    state_f[:, pl.ds(NODES, 8), :] = jnp.zeros((8, 8, 128), F32)
    contract(1)
    wait_sent(0)

    def section(r, _):
        def keep_value(n, value):
            X[r, n] = value

        unpack(r, False, keep_value)
        planes(r, (1, 2, 3, 4))
        width_inside(r)
        unpack(r, True, keep_value)
        planes(r, (0, 5))
        width_ends(r, True)
        settle(True)
        send(r + 1)
        width_ends(r, False)
        settle(False)
        weight = r.astype(F32)

        def gather(t, _):
            for v in range(24):
                n = t * 24 + v
                X[r + 1, n] = X[0, n] + weight * X[r, n] + T[n]
            return 0

        lax.fori_loop(0, 9, gather, 0)

        @pl.when(r == 0)
        def _():
            contract(0)

        wait_sent(r + 1)
        return 0

    lax.fori_loop(0, 2, section, 0)

    def emit(n, value):
        out_ref[pl.ds(n, 8, stride=NODES), :] = 0.5 * value

    for n in INTERIOR:
        emit(n, X[2, n])
    unpack(2, False, emit)
    unpack(2, True, emit)


def on_device(sizes, cost, states, rates, motion, drift, flags):
    elements = EX * EY * EZ
    hbm = pl.BlockSpec(memory_space=pltpu.HBM)
    operands = [
        pltpu.with_memory_space_constraint(x, pltpu.HBM)
        for x in (cost.reshape(8 * NODES, elements), states, rates, motion, drift, flags)
    ]
    tile = (8, 128)
    out = pl.pallas_call(
        functools.partial(kernel, sizes),
        out_shape=pltpu.VMEM((8 * NODES, elements), F32),
        in_specs=[hbm] * 6,
        out_specs=pl.BlockSpec(memory_space=pltpu.VMEM),
        scratch_shapes=[
            pltpu.SMEM((8,), F32),
            pltpu.SMEM((EX, EY), jnp.int32),
            pltpu.VMEM((8 * NODES, elements), F32),
            pltpu.VMEM((2, 8, NODES, elements), jnp.bfloat16),
            pltpu.VMEM((8, NODES + 8, elements), F32),
            pltpu.VMEM((8, 8, 8), F32),
            pltpu.VMEM((3, elements), F32),
            pltpu.VMEM((512, 256), jnp.bfloat16),
            pltpu.VMEM((2, NODES + 8, 64, 128), F32),
            pltpu.VMEM((3, NODES) + tile, F32),
            pltpu.VMEM((NODES,) + tile, F32),
            pltpu.VMEM((4,) + tile, F32),
            pltpu.VMEM((3, SEND_TILES) + tile, F32),
            pltpu.VMEM((3, RECV_TILES) + tile, F32),
            pltpu.VMEM((3, 8, 4, 128), F32),
            pltpu.VMEM((3, len(HALF_AT), 4, 128), F32),
            pltpu.SemaphoreType.DMA((3, 26)),
            pltpu.SemaphoreType.DMA((3, 26)),
            pltpu.SemaphoreType.DMA((6,)),
        ],
        compiler_params=pltpu.CompilerParams(
            collective_id=0, has_side_effects=True, vmem_limit_bytes=52 << 20
        ),
        name="adjoint_sections",
    )(*operands)
    return out.reshape(8, NODES, elements)


def solution(mesh):
    sizes = tuple(mesh.shape[axis] for axis in AXES)
    in_specs = (
        P(None, None, AXES),
        P(None, None, None, AXES),
        P(),
        P(None, AXES),
        P(),
        P("gx", "gy"),
    )
    return jax.shard_map(
        functools.partial(on_device, sizes),
        mesh=mesh,
        in_specs=in_specs,
        out_specs=P(None, None, AXES),
        check_vma=False,
    )
```

```python
import functools

import jax
import jax.numpy as jnp
import numpy as np
from jax import lax
from jax.experimental import pallas as pl
from jax.experimental.pallas import tpu as pltpu
from jax.sharding import PartitionSpec as P

EX = 2
EY = 8
EZ = 8
STEP_LENGTH = 0.05
AXES = ("gx", "gy", "gz")
STRIDES = (36, 6, 1)
MESH = pl.DeviceIdType.MESH
NODES = 216
F32 = jnp.float32


def derivative_numbers():
    points = np.array(
        [-1.0, -0.765055323929465, -0.285231516480645, 0.285231516480645, 0.765055323929465, 1.0]
    )
    legendre = (63.0 * points**5 - 70.0 * points**3 + 15.0 * points) / 8.0
    matrix = np.zeros((6, 6))
    for row_index in range(6):
        for col_index in range(6):
            if row_index != col_index:
                matrix[row_index, col_index] = (
                    legendre[row_index]
                    / legendre[col_index]
                    / (points[row_index] - points[col_index])
                )
    matrix[0, 0] = -7.5
    matrix[5, 5] = 7.5
    return matrix


DMAT = derivative_numbers()
EVEN = [[0.5 * float(DMAT[i, m] + DMAT[5 - i, m]) for m in range(3)] for i in range(3)]
ODD = [[0.5 * float(DMAT[i, m] - DMAT[5 - i, m]) for m in range(3)] for i in range(3)]

INNER = [(a, b) for a in range(1, 5) for b in range(1, 5)]
Y_GROUPS = [
    [(0, k) for k in range(6)] + INNER[0:2],
    [(5, k) for k in range(6)] + INNER[2:4],
    [(i, 0) for i in range(6)] + INNER[4:6],
    [(i, 5) for i in range(6)] + INNER[6:8],
    INNER[8:16],
]
REST = [(i, j) for i in range(1, 5) for j in range(6)]
Z_GROUPS = [
    [(0, j) for j in range(6)] + REST[0:2],
    [(5, j) for j in range(6)] + REST[2:4],
    REST[4:12],
    REST[12:20],
    REST[20:24],
]
X_HALVES = [(j, k) for j in range(5) for k in range(5)] + ["depth", "height", None]
X_TILES = 14
XL, XH, YL, YH, ZL, ZH, SEND_TILES = 0, 14, 28, 33, 38, 43, 48


def source_of(d):
    dx, dy, dz = d
    if dy == 0 and dz == 0:
        return (XL if dx < 0 else XH), X_TILES
    if dx == 0 and dz == 0:
        return (YL if dy < 0 else YH), 5
    if dx == 0 and dy == 0:
        return (ZL if dz < 0 else ZH), 5
    return (YL if dy < 0 else YH) + (2 if dz < 0 else 3), 1


def half_source_of(d):
    dx, dy, dz = d
    side = 0 if dx < 0 else 1
    if dy == 0:
        return 4 + 2 * (dz > 0) + side, (ZL if dz < 0 else ZH) + side
    return 2 * (dy > 0) + side, (YL if dy < 0 else YH) + side


def is_half(d):
    return d[0] != 0 and (d[1] != 0 or d[2] != 0)


def directions():
    every = [(x, y, z) for x in (-1, 0, 1) for y in (-1, 0, 1) for z in (-1, 0, 1) if (x, y, z) != (0, 0, 0)]

    def rank(d):
        count = sum(abs(v) for v in d)
        if count == 3:
            return 0
        if count == 2:
            return 1 if d[1] == 0 else (2 if d[2] == 0 else 3)
        return 4 if d[2] else (5 if d[1] else 6)

    return sorted(every, key=rank)


DIRECTIONS = directions()
RECV_AT = {}
RECV_TILES = 0
HALF_AT = {}
for _d in DIRECTIONS:
    if is_half(_d):
        HALF_AT[_d] = len(HALF_AT)
    else:
        RECV_AT[_d] = RECV_TILES
        RECV_TILES += source_of(_d)[1]


def pieces():
    table = {n: [] for n in range(NODES)}
    where = {h: (x // 2, 64 * (x % 2)) for x, h in enumerate(X_HALVES)}
    for f, base, p in ((1, 180, 1), (-1, 0, 0)):
        def add(j, k, half, shift, q, r):
            tile, across = where[half]
            table[base + j * 6 + k].append(((f, 0, 0), tile, across + shift, (p, q, r)))

        for j in range(5):
            for k in range(5):
                add(j, k, (j, k), 0, None, None)
        for t in range(5):
            add(5, t, (0, t), -8, "below", None)
            add(5, t, "depth", 8 * (7 - t), 7, None)
            add(t, 5, (t, 0), -1, None, "below")
            add(t, 5, "height", 7 - t, None, 7)
        add(5, 5, (0, 0), -9, "below", "below")
        add(5, 5, "depth", 8 * (7 - 5), 7, None)
        add(5, 5, "height", 7 - 8, "below", 7)
    for g, group in enumerate(Y_GROUPS):
        for s, (i, k) in enumerate(group):
            table[i * 36 + 30 + k].append(((0, 1, 0), g, 8 * (7 - s), (None, 7, None)))
            table[i * 36 + k].append(((0, -1, 0), g, -8 * s, (None, 0, None)))
    for g, group in enumerate(Z_GROUPS):
        for s, (i, j) in enumerate(group):
            table[i * 36 + j * 6 + 5].append(((0, 0, 1), g, 7 - s, (None, None, 7)))
            table[i * 36 + j * 6].append(((0, 0, -1), g, -s, (None, None, 0)))
    return table


HALF_FROM = dict(half_source_of(d) for d in DIRECTIONS if is_half(d))
PIECES = pieces()
BOUNDARY = [n for n in range(NODES) if PIECES[n]]
INTERIOR = [n for n in range(NODES) if not PIECES[n]]


def roll(x, shift):
    shift = shift % 128
    return x if shift == 0 else pltpu.roll(x, shift, 1)


def exists(d, sizes):
    ok = None
    for axis, off, size in zip(AXES, d, sizes):
        if off == 0:
            continue
        here = lax.axis_index(axis)
        term = here < size - 1 if off > 0 else here > 0
        ok = term if ok is None else jnp.logical_and(ok, term)
    return ok


def device_at(d):
    return {axis: lax.axis_index(axis) + off for axis, off in zip(AXES, d) if off != 0}


def kernel(
    sizes, cost_hbm, state_hbm, rates_hbm, motion_hbm, drift_hbm, flags_hbm, out_ref,
    drift_ref, flags_ref, stage, state_v, state_f, rates_v, motion_v, mix_lhs, mix, X, T, consts,
    send_buf, recv_buf, send_half, recv_half, send_sem, recv_sem, load_sem,
):
    lane = lax.broadcasted_iota(jnp.int32, (8, 128), 1)
    sub = lax.broadcasted_iota(jnp.int32, (8, 128), 0)
    p_at, q_at, r_at = lane // 64, (lane // 8) % 8, lane % 8

    barrier = pltpu.get_barrier_semaphore()
    for d in DIRECTIONS:
        @pl.when(exists(d, sizes))
        def _():
            pl.semaphore_signal(barrier, inc=1, device_id=device_at(d), device_id_type=MESH)

    loads = [
        pltpu.make_async_copy(cost_hbm, stage, load_sem.at[0]),
        pltpu.make_async_copy(motion_hbm, motion_v, load_sem.at[1]),
        pltpu.make_async_copy(rates_hbm, rates_v, load_sem.at[2]),
        pltpu.make_async_copy(state_hbm, state_v, load_sem.at[3]),
        pltpu.make_async_copy(drift_hbm, drift_ref, load_sem.at[4]),
        pltpu.make_async_copy(flags_hbm, flags_ref, load_sem.at[5]),
    ]
    for load in loads:
        load.start()

    for d in DIRECTIONS:
        @pl.when(jnp.logical_not(exists(tuple(-v for v in d), sizes)))
        def _():
            for s in range(3):
                if is_half(d):
                    recv_half[s, HALF_AT[d]] = jnp.zeros((4, 128), F32)
                else:
                    n = source_of(d)[1]
                    recv_buf[s, pl.ds(RECV_AT[d], n)] = jnp.zeros((n, 8, 128), F32)

    loads[5].wait()
    keep = jnp.ones((8, 128), F32)
    bottom = lax.axis_index("gz") == 0
    for p in range(EX):
        for q in range(EY):
            open_here = 1.0 - flags_ref[p, q].astype(F32)
            hit = jnp.logical_and(lane == p * 64 + q * 8, bottom)
            keep = jnp.where(hit, open_here, keep)
    consts[0] = keep

    def sweep(ref, d, needed):
        a_d, b_d = [x for x in range(3) if x != d]
        shift = (64, 8, 1)[d]
        at = (p_at, q_at, r_at)[d]
        last = (1, 7, 7)[d]

        for t in range(6):
            for u in range(6):
                if (t in (0, 5) or u in (0, 5)) != needed:
                    continue
                lo_n = t * STRIDES[a_d] + u * STRIDES[b_d]
                hi_n = lo_n + 5 * STRIDES[d]
                a, b = ref[lo_n], ref[hi_n]
                if d == 0:
                    both = jnp.where(at == 1, a, b)
                    both = both + roll(both, 64)
                    ref[lo_n] = jnp.where(at == 1, both, a)
                    ref[hi_n] = jnp.where(at == 0, both, b)
                else:
                    s = a + roll(b, shift)
                    ref[lo_n] = jnp.where(at > 0, s, a)
                    ref[hi_n] = jnp.where(at < last, roll(s, -shift), b)

    def pack_faces(slot):
        for g, group in enumerate(Y_GROUPS):
            low = high = jnp.zeros((8, 128), F32)
            for s, (i, k) in enumerate(group):
                low = jnp.where(q_at == s, roll(T[i * 36 + k], 8 * s), low)
                high = jnp.where(q_at == s, roll(T[i * 36 + 30 + k], 8 * (s - 7)), high)
            send_buf[slot, YL + g] = low
            send_buf[slot, YH + g] = high
        for g, group in enumerate(Z_GROUPS):
            low = high = jnp.zeros((8, 128), F32)
            for s, (i, j) in enumerate(group):
                low = jnp.where(r_at == s, roll(T[i * 36 + j * 6], s), low)
                high = jnp.where(r_at == s, roll(T[i * 36 + j * 6 + 5], s - 7), high)
            send_buf[slot, ZL + g] = low
            send_buf[slot, ZH + g] = high

        for at in range(8):
            full = send_buf[slot, HALF_FROM[at]]
            other = roll(pltpu.roll(full, 4, 0), 64)
            send_half[slot, at] = jnp.where(p_at == at % 2, full, other)[0:4]

    def pack_width(slot):
        def half(h, high):
            if h == "depth":
                return send_buf[slot, YH + high]
            if h == "height":
                return send_buf[slot, ZH + high]
            return T[180 * high + h[0] * 6 + h[1]]

        for t in range(X_TILES):
            for high, at in ((0, XL), (1, XH)):
                tile = roll(half(X_HALVES[2 * t], high), 64)
                if X_HALVES[2 * t + 1] is not None:
                    tile = jnp.where(p_at == 1 - high, tile, half(X_HALVES[2 * t + 1], high))
                send_buf[slot, at + t] = tile

    def message(slot, m):
        d = DIRECTIONS[m]
        if is_half(d):
            src = send_half.at[slot, half_source_of(d)[0]]
            dst = recv_half.at[slot, HALF_AT[d]]
        else:
            at, n = source_of(d)
            src = send_buf.at[slot, pl.ds(at, n)]
            dst = recv_buf.at[slot, pl.ds(RECV_AT[d], n)]
        return pltpu.make_async_remote_copy(
            src_ref=src,
            dst_ref=dst,
            send_sem=send_sem.at[slot, m],
            recv_sem=recv_sem.at[slot, m],
            device_id=device_at(d),
            device_id_type=MESH,
        )

    def start(slot, width):
        for m, d in enumerate(DIRECTIONS):
            if (d[1] == 0 and d[2] == 0) == width:
                @pl.when(exists(d, sizes))
                def _():
                    message(slot, m).start()

    def send(slot):
        pack_faces(slot)
        start(slot, False)
        pack_width(slot)
        start(slot, True)

    def wait_sent(slot):
        for m, d in enumerate(DIRECTIONS):
            @pl.when(exists(d, sizes))
            def _():
                message(slot, m).wait_send()

    def wait_received(slot, kind):
        for m, d in enumerate(DIRECTIONS):
            if (0 if d[0] == 0 else (1 if is_half(d) else 2)) == kind:
                @pl.when(exists(tuple(-v for v in d), sizes))
                def _():
                    message(slot, m).wait_recv()

    def got(slot, f, tile=0):
        return recv_buf[slot, RECV_AT[tuple(-v for v in f)] + tile]

    def got_half(slot, f):
        part = recv_half[slot, HALF_AT[tuple(-v for v in f)]]
        return jnp.concatenate([roll(part, 64), part], axis=0)

    def join(slot, across):
        zero = jnp.zeros((8, 128), F32)
        for fy in (1, -1):
            for g in (0, 1) if across else (2, 3):
                v = got(slot, (0, fy, 0), g)
                if g < 2:
                    fx = 1 if g == 1 else -1
                    mine = jnp.logical_and(p_at == (1 if fx > 0 else 0), q_at < 6)
                    v = v + jnp.where(mine, got_half(slot, (fx, fy, 0)), zero)
                    for fz in (1, -1):
                        target = (64 if fx > 0 else 0) + (47 if fz > 0 else 0)
                        origin = (0 if fx > 0 else 64) + (0 if fz > 0 else 47)
                        corner = roll(got_half(slot, (fx, fy, fz)), target - origin - 64)
                        v = v + jnp.where(lane == target, corner, zero)
                else:
                    fz = 1 if g == 3 else -1
                    v = jnp.where(jnp.logical_or(q_at == 0, q_at == 5), zero, v)
                    mine = jnp.logical_and(r_at == (7 if fz > 0 else 0), q_at < 6)
                    v = v + jnp.where(mine, roll(got(slot, (0, fy, fz)), 7 * fz), zero)
                recv_buf[slot, RECV_AT[(0, -fy, 0)] + g] = v
        for fz in (1, -1) if across else ():
            for g in range(2):
                fx = 1 if g == 1 else -1
                mine = jnp.logical_and(p_at == (1 if fx > 0 else 0), r_at < 6)
                v = got(slot, (0, 0, fz), g) + jnp.where(mine, got_half(slot, (fx, 0, fz)), zero)
                recv_buf[slot, RECV_AT[(0, 0, -fz)] + g] = v

    def masked(places):
        mask = None
        for at, place in zip((p_at, q_at, r_at), places):
            if place is not None:
                term = at < 7 if place == "below" else at == place
                mask = term if mask is None else jnp.logical_and(mask, term)
        return mask

    def unpack(slot, across, put):
        wait_received(slot, 1 if across else 0)
        join(slot, across)
        if across:
            wait_received(slot, 2)
        zero = jnp.zeros((8, 128), F32)
        for n in BOUNDARY:
            if (n // 36 in (0, 5)) != across:
                continue
            value = X[slot, n]
            for f, tile, shift, places in PIECES[n]:
                value = value + jnp.where(masked(places), roll(got(slot, f, tile), shift), zero)
            put(n, value)

    def line(r, base, d, add):
        stride = STRIDES[d]
        h = [X[r, base + m * stride] for m in range(6)]
        even = [h[i] + h[5 - i] for i in range(3)]
        odd = [h[i] - h[5 - i] for i in range(3)]
        speed = consts[1 + d]
        for m in range(3):
            pe = EVEN[0][m] * even[0] + EVEN[1][m] * even[1] + EVEN[2][m] * even[2]
            qo = ODD[0][m] * odd[0] + ODD[1][m] * odd[1] + ODD[2][m] * odd[2]
            for at, value in ((m, qo + pe), (5 - m, qo - pe)):
                n = base + at * stride
                value = speed * value
                if add:
                    value = value + T[n]
                if d == 2:
                    for a in range(8):
                        value = value + mix[1 - r, n, pl.ds(8 * a, 8), :] * X[r, n, pl.ds(a, 1), :]
                T[n] = value

    def planes(r, which):
        for d in (1, 2):
            for i in which:
                for t in range(6):
                    line(r, i * 36 + t * STRIDES[3 - d], d, d == 2 or i in (0, 5))

    def width_inside(r):
        speed = consts[1]
        for n in range(36):
            h = [X[r, n + 36 * i] for i in range(1, 5)]
            even, odd = (h[0] + h[3], h[1] + h[2]), (h[0] - h[3], h[1] - h[2])
            for m in range(3):
                pe = EVEN[1][m] * even[0] + EVEN[2][m] * even[1]
                qo = ODD[1][m] * odd[0] + ODD[2][m] * odd[1]
                for at, value in ((m, qo + pe), (5 - m, qo - pe)):
                    value = speed * value
                    T[n + 36 * at] = value if m == 0 else value + T[n + 36 * at]

    def width_ends(r, boundary):
        speed = consts[1]
        for j in range(6):
            for k in range(6):
                n = j * 6 + k
                whole = j in (0, 5) or k in (0, 5)
                if whole and not boundary:
                    continue
                first, last = X[r, n], X[r, n + 180]
                even, odd = speed * (first + last), speed * (first - last)
                for m in range(3):
                    if not whole and (m == 0) != boundary:
                        continue
                    pe, qo = EVEN[0][m] * even, ODD[0][m] * odd
                    for at, value in ((m, qo + pe), (5 - m, qo - pe)):
                        value = value + T[n + 36 * at]
                        T[n + 36 * at] = value * consts[0] if k == 0 else value

    def settle(needed):
        for d in range(3):
            sweep(T, d, needed)

    loads[1].wait()
    loads[4].wait()
    drift = jnp.zeros((8, 128), F32)
    for c in range(8):
        drift = jnp.where(sub == c, drift_ref[c], drift)
    for d in range(3):
        pace = jnp.broadcast_to(motion_v[pl.ds(d, 1), :], (8, 128))
        if d == 2:
            pace = pace + drift
        consts[1 + d] = -STEP_LENGTH * pace

    loads[0].wait()

    def fetch(t, _):
        for k in range(36):
            n = t * 36 + k
            v = stage[pl.ds(n, 8, stride=NODES), :]
            T[n] = v * keep if k % 6 == 0 else v
        return 0

    lax.fori_loop(0, 6, fetch, 0)
    settle(True)
    pack_faces(0)
    pack_width(0)
    count = 1
    for axis, size in zip(AXES, sizes):
        here = lax.axis_index(axis)
        count = count * (1 + (here > 0).astype(jnp.int32) + (here < size - 1).astype(jnp.int32))
    pl.semaphore_wait(barrier, count - 1)
    start(0, False)
    start(0, True)
    settle(False)

    def copy_over(t, _):
        for v in range(24):
            X[0, t * 24 + v] = T[t * 24 + v]
        return 0

    lax.fori_loop(0, 9, copy_over, 0)
    loads[2].wait()
    loads[3].wait()
    highest = lax.Precision.HIGHEST
    spread = (
        lax.broadcasted_iota(jnp.int32, (8, 256), 1) // 8 % 8
        == lax.broadcasted_iota(jnp.int32, (8, 256), 0)
    ).astype(F32)
    rows = []
    for a in range(8):
        block = rates_v[a]
        straight = jnp.dot(block, spread, precision=highest, preferred_element_type=F32)
        turned = lax.dot_general(
            block, spread, (((0,), (0,)), ((), ())), precision=highest, preferred_element_type=F32
        )
        rows.append(straight + turned)
    weights = STEP_LENGTH * jnp.concatenate(rows, axis=0)
    column = lax.broadcasted_iota(jnp.int32, (64, 256), 1)
    first = weights.astype(jnp.bfloat16).astype(F32)
    second = (weights - first).astype(jnp.bfloat16).astype(F32)
    third = (weights - first) - second
    parts = jnp.where(
        column < 64, first, jnp.where(column < 128, second, jnp.where(column < 192, third, 0.0))
    )
    for m in range(8):
        mix_lhs[pl.ds(64 * m, 64), :] = jnp.where(column % 8 == m, parts, 0.0).astype(jnp.bfloat16)

    def contract(s):
        for b in range(8):
            state_f[b, pl.ds(0, NODES)] = state_v[s, b].astype(F32)

        def body(g, _):
            base = pl.multiple_of(16 * g, 16)
            halves = []
            for half in range(2):
                block = state_f[:, pl.ds(base + 8 * half, 8), :]
                halves.append(block.reshape(64, 128).astype(jnp.bfloat16))
            both = jnp.concatenate(halves, axis=1)
            stacked = jnp.concatenate([both] * 4, axis=0)
            res = jnp.dot(mix_lhs[...], stacked, preferred_element_type=F32)
            for half in range(2):
                mix[s, pl.ds(base + 8 * half, 8)] = res[:, 128 * half : 128 * half + 128].reshape(8, 64, 128)
            return 0

        lax.fori_loop(0, 14, body, 0)

    state_f[:, pl.ds(NODES, 8), :] = jnp.zeros((8, 8, 128), F32)
    contract(1)
    wait_sent(0)

    def section(r, _):
        def keep_value(n, value):
            X[r, n] = value

        unpack(r, False, keep_value)
        planes(r, (1, 2, 3, 4))
        width_inside(r)
        unpack(r, True, keep_value)
        planes(r, (0, 5))
        width_ends(r, True)
        settle(True)
        send(r + 1)
        width_ends(r, False)
        settle(False)
        weight = r.astype(F32)

        def gather(t, _):
            for v in range(24):
                n = t * 24 + v
                X[r + 1, n] = X[0, n] + weight * X[r, n] + T[n]
            return 0

        lax.fori_loop(0, 9, gather, 0)

        @pl.when(r == 0)
        def _():
            contract(0)

        wait_sent(r + 1)
        return 0

    lax.fori_loop(0, 2, section, 0)

    def emit(n, value):
        out_ref[pl.ds(n, 8, stride=NODES), :] = 0.5 * value

    for n in INTERIOR:
        emit(n, X[2, n])
    unpack(2, False, emit)
    unpack(2, True, emit)


def on_device(sizes, cost, states, rates, motion, drift, flags):
    elements = EX * EY * EZ
    hbm = pl.BlockSpec(memory_space=pltpu.HBM)
    operands = [
        pltpu.with_memory_space_constraint(x, pltpu.HBM)
        for x in (cost.reshape(8 * NODES, elements), states, rates, motion, drift, flags)
    ]
    tile = (8, 128)
    out = pl.pallas_call(
        functools.partial(kernel, sizes),
        out_shape=pltpu.VMEM((8 * NODES, elements), F32),
        in_specs=[hbm] * 6,
        out_specs=pl.BlockSpec(memory_space=pltpu.VMEM),
        scratch_shapes=[
            pltpu.SMEM((8,), F32),
            pltpu.SMEM((EX, EY), jnp.int32),
            pltpu.VMEM((8 * NODES, elements), F32),
            pltpu.VMEM((2, 8, NODES, elements), jnp.bfloat16),
            pltpu.VMEM((8, NODES + 8, elements), F32),
            pltpu.VMEM((8, 8, 8), F32),
            pltpu.VMEM((3, elements), F32),
            pltpu.VMEM((512, 256), jnp.bfloat16),
            pltpu.VMEM((2, NODES + 8, 64, 128), F32),
            pltpu.VMEM((3, NODES) + tile, F32),
            pltpu.VMEM((NODES,) + tile, F32),
            pltpu.VMEM((4,) + tile, F32),
            pltpu.VMEM((3, SEND_TILES) + tile, F32),
            pltpu.VMEM((3, RECV_TILES) + tile, F32),
            pltpu.VMEM((3, 8, 4, 128), F32),
            pltpu.VMEM((3, len(HALF_AT), 4, 128), F32),
            pltpu.SemaphoreType.DMA((3, 26)),
            pltpu.SemaphoreType.DMA((3, 26)),
            pltpu.SemaphoreType.DMA((6,)),
        ],
        compiler_params=pltpu.CompilerParams(
            collective_id=0, has_side_effects=True, vmem_limit_bytes=52 << 20
        ),
        name="adjoint_sections",
    )(*operands)
    return out.reshape(8, NODES, elements)


def solution(mesh):
    sizes = tuple(mesh.shape[axis] for axis in AXES)
    in_specs = (
        P(None, None, AXES),
        P(None, None, None, AXES),
        P(),
        P(None, AXES),
        P(),
        P("gx", "gy"),
    )
    return jax.shard_map(
        functools.partial(on_device, sizes),
        mesh=mesh,
        in_specs=in_specs,
        out_specs=P(None, None, AXES),
        check_vma=False,
    )
```

```python
import functools

import jax
import jax.numpy as jnp
import numpy as np
from jax import lax
from jax.experimental import pallas as pl
from jax.experimental.pallas import tpu as pltpu
from jax.sharding import PartitionSpec as P

EX = 2
EY = 8
EZ = 8
STEP_LENGTH = 0.05
AXES = ("gx", "gy", "gz")
STRIDES = (36, 6, 1)
MESH = pl.DeviceIdType.MESH
NODES = 216
F32 = jnp.float32


def derivative_numbers():
    points = np.array(
        [-1.0, -0.765055323929465, -0.285231516480645, 0.285231516480645, 0.765055323929465, 1.0]
    )
    legendre = (63.0 * points**5 - 70.0 * points**3 + 15.0 * points) / 8.0
    matrix = np.zeros((6, 6))
    for row_index in range(6):
        for col_index in range(6):
            if row_index != col_index:
                matrix[row_index, col_index] = (
                    legendre[row_index]
                    / legendre[col_index]
                    / (points[row_index] - points[col_index])
                )
    matrix[0, 0] = -7.5
    matrix[5, 5] = 7.5
    return matrix


DMAT = derivative_numbers()
EVEN = [[0.5 * float(DMAT[i, m] + DMAT[5 - i, m]) for m in range(3)] for i in range(3)]
ODD = [[0.5 * float(DMAT[i, m] - DMAT[5 - i, m]) for m in range(3)] for i in range(3)]

INNER = [(a, b) for a in range(1, 5) for b in range(1, 5)]
Y_GROUPS = [
    [(0, k) for k in range(6)] + INNER[0:2],
    [(5, k) for k in range(6)] + INNER[2:4],
    [(i, 0) for i in range(6)] + INNER[4:6],
    [(i, 5) for i in range(6)] + INNER[6:8],
    INNER[8:16],
]
REST = [(i, j) for i in range(1, 5) for j in range(6)]
Z_GROUPS = [
    [(0, j) for j in range(6)] + REST[0:2],
    [(5, j) for j in range(6)] + REST[2:4],
    REST[4:12],
    REST[12:20],
    REST[20:24],
]
X_HALVES = [(j, k) for j in range(5) for k in range(5)] + ["depth", "height", None]
X_TILES = 14
XL, XH, YL, YH, ZL, ZH, SEND_TILES = 0, 14, 28, 33, 38, 43, 48


def source_of(d):
    dx, dy, dz = d
    if dy == 0 and dz == 0:
        return (XL if dx < 0 else XH), X_TILES
    if dx == 0 and dz == 0:
        return (YL if dy < 0 else YH), 5
    if dx == 0 and dy == 0:
        return (ZL if dz < 0 else ZH), 5
    return (YL if dy < 0 else YH) + (2 if dz < 0 else 3), 1


def half_source_of(d):
    dx, dy, dz = d
    side = 0 if dx < 0 else 1
    if dy == 0:
        return 4 + 2 * (dz > 0) + side, (ZL if dz < 0 else ZH) + side
    return 2 * (dy > 0) + side, (YL if dy < 0 else YH) + side


def is_half(d):
    return d[0] != 0 and (d[1] != 0 or d[2] != 0)


def directions():
    every = [(x, y, z) for x in (-1, 0, 1) for y in (-1, 0, 1) for z in (-1, 0, 1) if (x, y, z) != (0, 0, 0)]

    def rank(d):
        count = sum(abs(v) for v in d)
        if count == 3:
            return 0
        if count == 2:
            return 1 if d[1] == 0 else (2 if d[2] == 0 else 3)
        return 5 if d[2] else (4 if d[1] else 6)

    return sorted(every, key=rank)


DIRECTIONS = directions()
RECV_AT = {}
RECV_TILES = 0
HALF_AT = {}
for _d in DIRECTIONS:
    if is_half(_d):
        HALF_AT[_d] = len(HALF_AT)
    else:
        RECV_AT[_d] = RECV_TILES
        RECV_TILES += source_of(_d)[1]


def pieces():
    table = {n: [] for n in range(NODES)}
    where = {h: (x // 2, 64 * (x % 2)) for x, h in enumerate(X_HALVES)}
    for f, base, p in ((1, 180, 1), (-1, 0, 0)):
        def add(j, k, half, shift, q, r):
            tile, across = where[half]
            table[base + j * 6 + k].append(((f, 0, 0), tile, across + shift, (p, q, r)))

        for j in range(5):
            for k in range(5):
                add(j, k, (j, k), 0, None, None)
        for t in range(5):
            add(5, t, (0, t), -8, "below", None)
            add(5, t, "depth", 8 * (7 - t), 7, None)
            add(t, 5, (t, 0), -1, None, "below")
            add(t, 5, "height", 7 - t, None, 7)
        add(5, 5, (0, 0), -9, "below", "below")
        add(5, 5, "depth", 8 * (7 - 5), 7, None)
        add(5, 5, "height", 7 - 8, "below", 7)
    for g, group in enumerate(Y_GROUPS):
        for s, (i, k) in enumerate(group):
            table[i * 36 + 30 + k].append(((0, 1, 0), g, 8 * (7 - s), (None, 7, None)))
            table[i * 36 + k].append(((0, -1, 0), g, -8 * s, (None, 0, None)))
    for g, group in enumerate(Z_GROUPS):
        for s, (i, j) in enumerate(group):
            table[i * 36 + j * 6 + 5].append(((0, 0, 1), g, 7 - s, (None, None, 7)))
            table[i * 36 + j * 6].append(((0, 0, -1), g, -s, (None, None, 0)))
    return table


HALF_FROM = dict(half_source_of(d) for d in DIRECTIONS if is_half(d))
PIECES = pieces()
BOUNDARY = [n for n in range(NODES) if PIECES[n]]
INTERIOR = [n for n in range(NODES) if not PIECES[n]]


def roll(x, shift):
    shift = shift % 128
    return x if shift == 0 else pltpu.roll(x, shift, 1)


def exists(d, sizes):
    ok = None
    for axis, off, size in zip(AXES, d, sizes):
        if off == 0:
            continue
        here = lax.axis_index(axis)
        term = here < size - 1 if off > 0 else here > 0
        ok = term if ok is None else jnp.logical_and(ok, term)
    return ok


def device_at(d):
    return {axis: lax.axis_index(axis) + off for axis, off in zip(AXES, d) if off != 0}


def kernel(
    sizes, cost_hbm, state_hbm, rates_hbm, motion_hbm, drift_hbm, flags_hbm, out_ref,
    drift_ref, flags_ref, stage, state_v, state_f, rates_v, motion_v, mix_lhs, mix, X, T, consts,
    send_buf, recv_buf, send_half, recv_half, send_sem, recv_sem, load_sem,
):
    lane = lax.broadcasted_iota(jnp.int32, (8, 128), 1)
    sub = lax.broadcasted_iota(jnp.int32, (8, 128), 0)
    p_at, q_at, r_at = lane // 64, (lane // 8) % 8, lane % 8

    barrier = pltpu.get_barrier_semaphore()
    for d in DIRECTIONS:
        @pl.when(exists(d, sizes))
        def _():
            pl.semaphore_signal(barrier, inc=1, device_id=device_at(d), device_id_type=MESH)

    loads = [
        pltpu.make_async_copy(cost_hbm, stage, load_sem.at[0]),
        pltpu.make_async_copy(motion_hbm, motion_v, load_sem.at[1]),
        pltpu.make_async_copy(rates_hbm, rates_v, load_sem.at[2]),
        pltpu.make_async_copy(state_hbm, state_v, load_sem.at[3]),
        pltpu.make_async_copy(drift_hbm, drift_ref, load_sem.at[4]),
        pltpu.make_async_copy(flags_hbm, flags_ref, load_sem.at[5]),
    ]
    for load in loads:
        load.start()

    for d in DIRECTIONS:
        @pl.when(jnp.logical_not(exists(tuple(-v for v in d), sizes)))
        def _():
            for s in range(3):
                if is_half(d):
                    recv_half[s, HALF_AT[d]] = jnp.zeros((4, 128), F32)
                else:
                    n = source_of(d)[1]
                    recv_buf[s, pl.ds(RECV_AT[d], n)] = jnp.zeros((n, 8, 128), F32)

    loads[5].wait()
    keep = jnp.ones((8, 128), F32)
    bottom = lax.axis_index("gz") == 0
    for p in range(EX):
        for q in range(EY):
            open_here = 1.0 - flags_ref[p, q].astype(F32)
            hit = jnp.logical_and(lane == p * 64 + q * 8, bottom)
            keep = jnp.where(hit, open_here, keep)
    consts[0] = keep

    def sweep(ref, d, needed):
        a_d, b_d = [x for x in range(3) if x != d]
        shift = (64, 8, 1)[d]
        at = (p_at, q_at, r_at)[d]
        last = (1, 7, 7)[d]

        for t in range(6):
            for u in range(6):
                if (t in (0, 5) or u in (0, 5)) != needed:
                    continue
                lo_n = t * STRIDES[a_d] + u * STRIDES[b_d]
                hi_n = lo_n + 5 * STRIDES[d]
                a, b = ref[lo_n], ref[hi_n]
                if d == 0:
                    both = jnp.where(at == 1, a, b)
                    both = both + roll(both, 64)
                    ref[lo_n] = jnp.where(at == 1, both, a)
                    ref[hi_n] = jnp.where(at == 0, both, b)
                else:
                    s = a + roll(b, shift)
                    ref[lo_n] = jnp.where(at > 0, s, a)
                    ref[hi_n] = jnp.where(at < last, roll(s, -shift), b)

    def pack_faces(slot):
        for g, group in enumerate(Y_GROUPS):
            low = high = jnp.zeros((8, 128), F32)
            for s, (i, k) in enumerate(group):
                low = jnp.where(q_at == s, roll(T[i * 36 + k], 8 * s), low)
                high = jnp.where(q_at == s, roll(T[i * 36 + 30 + k], 8 * (s - 7)), high)
            send_buf[slot, YL + g] = low
            send_buf[slot, YH + g] = high
        for g, group in enumerate(Z_GROUPS):
            low = high = jnp.zeros((8, 128), F32)
            for s, (i, j) in enumerate(group):
                low = jnp.where(r_at == s, roll(T[i * 36 + j * 6], s), low)
                high = jnp.where(r_at == s, roll(T[i * 36 + j * 6 + 5], s - 7), high)
            send_buf[slot, ZL + g] = low
            send_buf[slot, ZH + g] = high

        for at in range(8):
            full = send_buf[slot, HALF_FROM[at]]
            other = roll(pltpu.roll(full, 4, 0), 64)
            send_half[slot, at] = jnp.where(p_at == at % 2, full, other)[0:4]

    def pack_width(slot):
        def half(h, high):
            if h == "depth":
                return send_buf[slot, YH + high]
            if h == "height":
                return send_buf[slot, ZH + high]
            return T[180 * high + h[0] * 6 + h[1]]

        for t in range(X_TILES):
            for high, at in ((0, XL), (1, XH)):
                tile = roll(half(X_HALVES[2 * t], high), 64)
                if X_HALVES[2 * t + 1] is not None:
                    tile = jnp.where(p_at == 1 - high, tile, half(X_HALVES[2 * t + 1], high))
                send_buf[slot, at + t] = tile

    def message(slot, m):
        d = DIRECTIONS[m]
        if is_half(d):
            src = send_half.at[slot, half_source_of(d)[0]]
            dst = recv_half.at[slot, HALF_AT[d]]
        else:
            at, n = source_of(d)
            src = send_buf.at[slot, pl.ds(at, n)]
            dst = recv_buf.at[slot, pl.ds(RECV_AT[d], n)]
        return pltpu.make_async_remote_copy(
            src_ref=src,
            dst_ref=dst,
            send_sem=send_sem.at[slot, m],
            recv_sem=recv_sem.at[slot, m],
            device_id=device_at(d),
            device_id_type=MESH,
        )

    def start(slot, width):
        for m, d in enumerate(DIRECTIONS):
            if (d[1] == 0 and d[2] == 0) == width:
                @pl.when(exists(d, sizes))
                def _():
                    message(slot, m).start()

    def send(slot):
        pack_faces(slot)
        pack_width(slot)
        start(slot, False)
        start(slot, True)

    def wait_sent(slot):
        for m, d in enumerate(DIRECTIONS):
            @pl.when(exists(d, sizes))
            def _():
                message(slot, m).wait_send()

    def wait_received(slot, kind):
        for m, d in enumerate(DIRECTIONS):
            if (0 if d[0] == 0 else (1 if is_half(d) else 2)) == kind:
                @pl.when(exists(tuple(-v for v in d), sizes))
                def _():
                    message(slot, m).wait_recv()

    def got(slot, f, tile=0):
        return recv_buf[slot, RECV_AT[tuple(-v for v in f)] + tile]

    def got_half(slot, f):
        part = recv_half[slot, HALF_AT[tuple(-v for v in f)]]
        return jnp.concatenate([roll(part, 64), part], axis=0)

    def join(slot, across):
        zero = jnp.zeros((8, 128), F32)
        for fy in (1, -1):
            for g in (0, 1) if across else (2, 3):
                v = got(slot, (0, fy, 0), g)
                if g < 2:
                    fx = 1 if g == 1 else -1
                    mine = jnp.logical_and(p_at == (1 if fx > 0 else 0), q_at < 6)
                    v = v + jnp.where(mine, got_half(slot, (fx, fy, 0)), zero)
                    for fz in (1, -1):
                        target = (64 if fx > 0 else 0) + (47 if fz > 0 else 0)
                        origin = (0 if fx > 0 else 64) + (0 if fz > 0 else 47)
                        corner = roll(got_half(slot, (fx, fy, fz)), target - origin - 64)
                        v = v + jnp.where(lane == target, corner, zero)
                else:
                    fz = 1 if g == 3 else -1
                    v = jnp.where(jnp.logical_or(q_at == 0, q_at == 5), zero, v)
                    mine = jnp.logical_and(r_at == (7 if fz > 0 else 0), q_at < 6)
                    v = v + jnp.where(mine, roll(got(slot, (0, fy, fz)), 7 * fz), zero)
                recv_buf[slot, RECV_AT[(0, -fy, 0)] + g] = v
        for fz in (1, -1) if across else ():
            for g in range(2):
                fx = 1 if g == 1 else -1
                mine = jnp.logical_and(p_at == (1 if fx > 0 else 0), r_at < 6)
                v = got(slot, (0, 0, fz), g) + jnp.where(mine, got_half(slot, (fx, 0, fz)), zero)
                recv_buf[slot, RECV_AT[(0, 0, -fz)] + g] = v

    def masked(places):
        mask = None
        for at, place in zip((p_at, q_at, r_at), places):
            if place is not None:
                term = at < 7 if place == "below" else at == place
                mask = term if mask is None else jnp.logical_and(mask, term)
        return mask

    def unpack(slot, across, put):
        wait_received(slot, 1 if across else 0)
        join(slot, across)
        if across:
            wait_received(slot, 2)
        zero = jnp.zeros((8, 128), F32)
        for n in BOUNDARY:
            if (n // 36 in (0, 5)) != across:
                continue
            value = X[slot, n]
            for f, tile, shift, places in PIECES[n]:
                value = value + jnp.where(masked(places), roll(got(slot, f, tile), shift), zero)
            put(n, value)

    def line(r, base, d, add):
        stride = STRIDES[d]
        h = [X[r, base + m * stride] for m in range(6)]
        even = [h[i] + h[5 - i] for i in range(3)]
        odd = [h[i] - h[5 - i] for i in range(3)]
        speed = consts[1 + d]
        for m in range(3):
            pe = EVEN[0][m] * even[0] + EVEN[1][m] * even[1] + EVEN[2][m] * even[2]
            qo = ODD[0][m] * odd[0] + ODD[1][m] * odd[1] + ODD[2][m] * odd[2]
            for at, value in ((m, qo + pe), (5 - m, qo - pe)):
                n = base + at * stride
                value = speed * value
                if add:
                    value = value + T[n]
                if d == 2:
                    for a in range(8):
                        value = value + mix[1 - r, n, pl.ds(8 * a, 8), :] * X[r, n, pl.ds(a, 1), :]
                T[n] = value

    def planes(r, which):
        for d in (1, 2):
            for i in which:
                for t in range(6):
                    line(r, i * 36 + t * STRIDES[3 - d], d, d == 2 or i in (0, 5))

    def width_inside(r):
        speed = consts[1]
        for n in range(36):
            h = [X[r, n + 36 * i] for i in range(1, 5)]
            even, odd = (h[0] + h[3], h[1] + h[2]), (h[0] - h[3], h[1] - h[2])
            for m in range(3):
                pe = EVEN[1][m] * even[0] + EVEN[2][m] * even[1]
                qo = ODD[1][m] * odd[0] + ODD[2][m] * odd[1]
                for at, value in ((m, qo + pe), (5 - m, qo - pe)):
                    value = speed * value
                    T[n + 36 * at] = value if m == 0 else value + T[n + 36 * at]

    def width_ends(r, boundary):
        speed = consts[1]
        for j in range(6):
            for k in range(6):
                n = j * 6 + k
                whole = j in (0, 5) or k in (0, 5)
                if whole and not boundary:
                    continue
                first, last = X[r, n], X[r, n + 180]
                even, odd = speed * (first + last), speed * (first - last)
                for m in range(3):
                    if not whole and (m == 0) != boundary:
                        continue
                    pe, qo = EVEN[0][m] * even, ODD[0][m] * odd
                    for at, value in ((m, qo + pe), (5 - m, qo - pe)):
                        value = value + T[n + 36 * at]
                        T[n + 36 * at] = value * consts[0] if k == 0 else value

    def settle(needed):
        for d in range(3):
            sweep(T, d, needed)

    loads[1].wait()
    loads[4].wait()
    drift = jnp.zeros((8, 128), F32)
    for c in range(8):
        drift = jnp.where(sub == c, drift_ref[c], drift)
    for d in range(3):
        pace = jnp.broadcast_to(motion_v[pl.ds(d, 1), :], (8, 128))
        if d == 2:
            pace = pace + drift
        consts[1 + d] = -STEP_LENGTH * pace

    loads[0].wait()

    def fetch(t, _):
        for k in range(36):
            n = t * 36 + k
            v = stage[pl.ds(n, 8, stride=NODES), :]
            T[n] = v * keep if k % 6 == 0 else v
        return 0

    lax.fori_loop(0, 6, fetch, 0)
    settle(True)
    pack_faces(0)
    pack_width(0)
    count = 1
    for axis, size in zip(AXES, sizes):
        here = lax.axis_index(axis)
        count = count * (1 + (here > 0).astype(jnp.int32) + (here < size - 1).astype(jnp.int32))
    pl.semaphore_wait(barrier, count - 1)
    start(0, False)
    start(0, True)
    settle(False)

    def copy_over(t, _):
        for v in range(24):
            X[0, t * 24 + v] = T[t * 24 + v]
        return 0

    lax.fori_loop(0, 9, copy_over, 0)
    loads[2].wait()
    loads[3].wait()
    highest = lax.Precision.HIGHEST
    spread = (
        lax.broadcasted_iota(jnp.int32, (8, 256), 1) // 8 % 8
        == lax.broadcasted_iota(jnp.int32, (8, 256), 0)
    ).astype(F32)
    rows = []
    for a in range(8):
        block = rates_v[a]
        straight = jnp.dot(block, spread, precision=highest, preferred_element_type=F32)
        turned = lax.dot_general(
            block, spread, (((0,), (0,)), ((), ())), precision=highest, preferred_element_type=F32
        )
        rows.append(straight + turned)
    weights = STEP_LENGTH * jnp.concatenate(rows, axis=0)
    column = lax.broadcasted_iota(jnp.int32, (64, 256), 1)
    first = weights.astype(jnp.bfloat16).astype(F32)
    second = (weights - first).astype(jnp.bfloat16).astype(F32)
    third = (weights - first) - second
    parts = jnp.where(
        column < 64, first, jnp.where(column < 128, second, jnp.where(column < 192, third, 0.0))
    )
    for m in range(8):
        mix_lhs[pl.ds(64 * m, 64), :] = jnp.where(column % 8 == m, parts, 0.0).astype(jnp.bfloat16)

    def contract(s):
        for b in range(8):
            state_f[b, pl.ds(0, NODES)] = state_v[s, b].astype(F32)

        def body(g, _):
            base = pl.multiple_of(16 * g, 16)
            halves = []
            for half in range(2):
                block = state_f[:, pl.ds(base + 8 * half, 8), :]
                halves.append(block.reshape(64, 128).astype(jnp.bfloat16))
            both = jnp.concatenate(halves, axis=1)
            stacked = jnp.concatenate([both] * 4, axis=0)
            res = jnp.dot(mix_lhs[...], stacked, preferred_element_type=F32)
            for half in range(2):
                mix[s, pl.ds(base + 8 * half, 8)] = res[:, 128 * half : 128 * half + 128].reshape(8, 64, 128)
            return 0

        lax.fori_loop(0, 14, body, 0)

    state_f[:, pl.ds(NODES, 8), :] = jnp.zeros((8, 8, 128), F32)
    contract(1)
    wait_sent(0)

    def section(r, _):
        def keep_value(n, value):
            X[r, n] = value

        unpack(r, False, keep_value)
        planes(r, (1, 2, 3, 4))
        width_inside(r)
        unpack(r, True, keep_value)
        planes(r, (0, 5))
        width_ends(r, True)
        settle(True)
        send(r + 1)
        width_ends(r, False)
        settle(False)
        weight = r.astype(F32)

        def gather(t, _):
            for v in range(24):
                n = t * 24 + v
                X[r + 1, n] = X[0, n] + weight * X[r, n] + T[n]
            return 0

        lax.fori_loop(0, 9, gather, 0)

        @pl.when(r == 0)
        def _():
            contract(0)

        wait_sent(r + 1)
        return 0

    lax.fori_loop(0, 2, section, 0)

    def emit(n, value):
        out_ref[pl.ds(n, 8, stride=NODES), :] = 0.5 * value

    for n in INTERIOR:
        emit(n, X[2, n])
    unpack(2, False, emit)
    unpack(2, True, emit)


def on_device(sizes, cost, states, rates, motion, drift, flags):
    elements = EX * EY * EZ
    hbm = pl.BlockSpec(memory_space=pltpu.HBM)
    operands = [
        pltpu.with_memory_space_constraint(x, pltpu.HBM)
        for x in (cost.reshape(8 * NODES, elements), states, rates, motion, drift, flags)
    ]
    tile = (8, 128)
    out = pl.pallas_call(
        functools.partial(kernel, sizes),
        out_shape=pltpu.VMEM((8 * NODES, elements), F32),
        in_specs=[hbm] * 6,
        out_specs=pl.BlockSpec(memory_space=pltpu.VMEM),
        scratch_shapes=[
            pltpu.SMEM((8,), F32),
            pltpu.SMEM((EX, EY), jnp.int32),
            pltpu.VMEM((8 * NODES, elements), F32),
            pltpu.VMEM((2, 8, NODES, elements), jnp.bfloat16),
            pltpu.VMEM((8, NODES + 8, elements), F32),
            pltpu.VMEM((8, 8, 8), F32),
            pltpu.VMEM((3, elements), F32),
            pltpu.VMEM((512, 256), jnp.bfloat16),
            pltpu.VMEM((2, NODES + 8, 64, 128), F32),
            pltpu.VMEM((3, NODES) + tile, F32),
            pltpu.VMEM((NODES,) + tile, F32),
            pltpu.VMEM((4,) + tile, F32),
            pltpu.VMEM((3, SEND_TILES) + tile, F32),
            pltpu.VMEM((3, RECV_TILES) + tile, F32),
            pltpu.VMEM((3, 8, 4, 128), F32),
            pltpu.VMEM((3, len(HALF_AT), 4, 128), F32),
            pltpu.SemaphoreType.DMA((3, 26)),
            pltpu.SemaphoreType.DMA((3, 26)),
            pltpu.SemaphoreType.DMA((6,)),
        ],
        compiler_params=pltpu.CompilerParams(
            collective_id=0, has_side_effects=True, vmem_limit_bytes=52 << 20
        ),
        name="adjoint_sections",
    )(*operands)
    return out.reshape(8, NODES, elements)


def solution(mesh):
    sizes = tuple(mesh.shape[axis] for axis in AXES)
    in_specs = (
        P(None, None, AXES),
        P(None, None, None, AXES),
        P(),
        P(None, AXES),
        P(),
        P("gx", "gy"),
    )
    return jax.shard_map(
        functools.partial(on_device, sizes),
        mesh=mesh,
        in_specs=in_specs,
        out_specs=P(None, None, AXES),
        check_vma=False,
    )
```
